32 devices in a mesh: grp: 2 (over x), fiber: 8 (over z, y), tm: 2 (over core).
Axes of the slice: x: 2, y: 2, z: 4, core: 2. Of those that a mesh axis runs over, the one named last changes fastest.
Arguments:
- samples: bfloat16 [64, 5120, 128], P('tm', ('grp', 'fiber')), parts along dimension 1, may hold values from -6 to 6
- counts: int32 [16], P(('grp', 'fiber')), parts along dimension 0, may hold values from 80 to 320
- reach_limit: int32 [5120], P(('grp', 'fiber')), parts along dimension 0, may hold values from 320 to 960
Outputs:
- coherence_real: bfloat16 [32, 5120, 960], P('tm', ('grp', 'fiber')), parts along dimension 1
- coherence_imag: bfloat16 [32, 5120, 960], P('tm', ('grp', 'fiber')), parts along dimension 1
The draws below stay inside these ranges and needn't reach their ends.
There are 2 independent parts, one for each index of `grp`. The reference program is written for one: setup_inputs(seed, part) draws one part's arguments, and reference() takes and returns one part's arrays. A program takes and returns all parts, laid end to end along the dimension named above; each array names one. Nothing has to cross between parts.
All inputs are finite; a program needn't handle non-finite values.
Results may differ from the reference program's by a relative error of at most 0.0069.
Values may be sent and summed in bfloat16 or wider, within the bound.
No kernel may reach another device: no remote copies, remote signals or barrier semaphores. Data moves between devices by JAX's collectives and lax.ppermute only.
A program may use at most 576 MiB of HBM per device.

```python
import math
import jax
import jax.numpy as jnp
from jax import lax

FREQS = 32
SAMPLES = 128
FIRST_BIN = 8
CB = 320
WINDOWS = 64
CHANNELS = 2560
N_FIBER = 8


def place_ends(entries, rng, smallest, high):
    spot = [jax.random.randint(jax.random.fold_in(rng, axis), (), 0, length) for axis, length in enumerate(entries.shape)]
    widest = entries.shape.index(max(entries.shape))
    beside = spot[:widest] + [(spot[widest] + 1) % entries.shape[widest]] + spot[widest + 1:]
    return entries.at[tuple(spot)].set(smallest).at[tuple(beside)].set(high)


def block_scale(key, extent, pieces, least, top_value):
    loudness = 1.0
    for axis_at, blocks in pieces:
        draws = jax.random.uniform(jax.random.fold_in(jax.random.fold_in(key, 6), axis_at), (blocks,), jnp.float32, least / len(pieces), top_value / len(pieces))
        loudness = loudness * jnp.repeat(jnp.exp(draws), extent[axis_at] // blocks).reshape((-1,) + (1,) * (len(extent) - 1 - axis_at))
    return loudness


def bell_draw(own_key, extent, width, most, split=(), kind=jnp.bfloat16):
    factor_of = block_scale(own_key, extent, split, -0.22, 0.18) if split else 1.0
    values = jax.random.normal(own_key, extent, jnp.float32) * width * factor_of
    return jnp.minimum(jnp.maximum(values, -most), most).astype(kind)


def setup_inputs(seed: int = 0, part: int = 0) -> dict:
    seeds = jax.random.split(jax.random.key(seed), 4)
    part_keys = jax.random.split(jax.random.fold_in(seeds[3], part), 4)
    return {
        "samples": bell_draw(part_keys[0], (WINDOWS, CHANNELS, SAMPLES), 1.0, 6.0, ((0, 2), (1, 8))),
        "counts": place_ends(jax.random.randint(part_keys[1], (N_FIBER,), CB // 4, CB + 1), jax.random.fold_in(part_keys[1], 1), CB // 4, CB).astype(jnp.int32),
        "reach_limit": place_ends(jax.random.randint(part_keys[2], (CHANNELS,), CB, 3 * CB + 1), jax.random.fold_in(part_keys[2], 1), CB, 3 * CB).astype(jnp.int32),
    }


def make_table(length, bins, first_bin):
    steps_index = jnp.arange(length, dtype=jnp.int32)
    bin_index = jnp.arange(bins, dtype=jnp.int32) + first_bin
    products = steps_index[:, None] * bin_index[None, :] % length
    phases = 2.0 * math.pi * products.astype(jnp.float32) / length
    taper = 0.5 - 0.5 * jnp.cos(2.0 * math.pi * steps_index.astype(jnp.float32) / length)
    cosines = taper[:, None] * jnp.cos(phases)
    sines = -taper[:, None] * jnp.sin(phases)
    return jnp.concatenate([cosines, sines], axis=1).astype(jnp.bfloat16)

def diagonal_band(matrix):
    bins_here, rows, columns = matrix.shape
    flattened = matrix.reshape(bins_here, rows * columns)
    flattened = jnp.pad(flattened, ((0, 0), (0, rows)))
    return flattened.reshape(bins_here, rows, columns + 1)[:, :, 1:columns - rows + 1]

def reference(samples, counts, reach_limit):
    dft_table = make_table(SAMPLES, FREQS, FIRST_BIN)
    raw_spectra = jnp.einsum('wcl,lg->gwc', samples.astype(jnp.float32), dft_table.astype(jnp.float32))
    real_raw = raw_spectra[:FREQS]
    imag_raw = raw_spectra[FREQS:]
    level = lax.optimization_barrier(jnp.mean(real_raw * real_raw + imag_raw * imag_raw, axis=0))
    scale = lax.rsqrt(level + 1e-06)
    channel = jnp.arange(CHANNELS, dtype=jnp.int32)
    active = (channel % CB < counts[channel // CB]).astype(jnp.float32)
    real_part = (real_raw * scale * active).astype(jnp.bfloat16)
    imag_part = (imag_raw * scale * active).astype(jnp.bfloat16)
    real_wide = jnp.pad(real_part, ((0, 0), (0, 0), (0, 3 * CB))).astype(jnp.float32)
    imag_wide = jnp.pad(imag_part, ((0, 0), (0, 0), (0, 3 * CB))).astype(jnp.float32)
    power_sum = lax.optimization_barrier(jnp.sum(real_wide * real_wide + imag_wide * imag_wide, axis=1))
    inverse_root = lax.rsqrt(power_sum / WINDOWS + 1e-06)

    def per_block(block_index):
        start = (block_index * CB).astype(jnp.int32)
        left_real = lax.dynamic_slice_in_dim(real_wide, start, CB, 2)
        left_imag = lax.dynamic_slice_in_dim(imag_wide, start, CB, 2)
        right_real = lax.dynamic_slice_in_dim(real_wide, start, 4 * CB, 2)
        right_imag = lax.dynamic_slice_in_dim(imag_wide, start, 4 * CB, 2)
        cross_real = jnp.einsum('fwc,fwj->fcj', left_real, right_real) + jnp.einsum('fwc,fwj->fcj', left_imag, right_imag)
        cross_imag = jnp.einsum('fwc,fwj->fcj', left_imag, right_real) - jnp.einsum('fwc,fwj->fcj', left_real, right_imag)
        band_real = diagonal_band(cross_real)
        band_imag = diagonal_band(cross_imag)
        roots_right = lax.dynamic_slice_in_dim(inverse_root, start, 4 * CB, 1)
        own_scale = roots_right[:, :CB]
        partner = diagonal_band(jnp.broadcast_to(roots_right[:, None, :], (FREQS, CB, 4 * CB)))
        limits = lax.dynamic_slice_in_dim(reach_limit, start, CB, 0)
        offsets = jnp.arange(1, 3 * CB + 1, dtype=jnp.int32)
        in_reach = (offsets[None, :] <= limits[:, None]).astype(jnp.float32)
        factor = own_scale[:, :, None] * partner * in_reach[None, :, :] / math.sqrt(WINDOWS)
        return ((band_real * factor).astype(jnp.bfloat16), (band_imag * factor).astype(jnp.bfloat16))
    outputs = lax.map(per_block, jnp.arange(CHANNELS // CB, dtype=jnp.int32))
    coherence_real = outputs[0].transpose(1, 0, 2, 3).reshape(FREQS, CHANNELS, 3 * CB)
    coherence_imag = outputs[1].transpose(1, 0, 2, 3).reshape(FREQS, CHANNELS, 3 * CB)
    return (coherence_real, coherence_imag)
```

```python
import functools
import math

import jax
import jax.numpy as jnp
import ml_dtypes
import numpy as np
from jax import lax
from jax.experimental import pallas as pl
from jax.experimental.pallas import tpu as pltpu
from jax.sharding import PartitionSpec as P

FREQS = 32
FIRST_BIN = 8
LANES = 128
HOPS = 3
ROWS = 64
CHUNKS = 4


def make_table(length, bins, first_bin):
    steps_index = np.arange(length, dtype=np.int32)
    bin_index = np.arange(bins, dtype=np.int32) + first_bin
    products = bin_index[:, None] * steps_index[None, :] % length
    phases = (2.0 * math.pi * products / length).astype(np.float32)
    taper = 0.5 - 0.5 * np.cos((2.0 * math.pi * steps_index / length).astype(np.float32))
    taper = taper.astype(np.float32)
    cosines = taper[None, :] * np.cos(phases)
    sines = -taper[None, :] * np.sin(phases)
    return np.concatenate([cosines, sines], axis=0).astype(ml_dtypes.bfloat16)


def spectra_kernel(place_ref, samples_ref, table_ref, mine_ref, other_ref, raw_ref):
    windows, block, _ = samples_ref.shape
    pairs = mine_ref.shape[0]
    here = place_ref[0]
    tiles = raw_ref.shape[0]
    channel = lax.broadcasted_iota(jnp.int32, (1, block), 1)
    active = (channel < place_ref[1]).astype(jnp.float32)
    for w in range(windows):
        raw = lax.dot_general(
            table_ref[...], samples_ref[w], (((1,), (1,)), ((), ())),
            preferred_element_type=jnp.float32,
        )
        level = jnp.sum(raw * raw, axis=0, keepdims=True) * (1.0 / FREQS)
        white = raw * (lax.rsqrt(level + 1e-06) * active)
        for tile in range(tiles):
            start = tile * LANES
            width = min(LANES, block - start)
            raw_ref[tile, w * 2 * FREQS : (w + 1) * 2 * FREQS, :width] = white[:, start : start + width]
    for out_ref, first in ((mine_ref, here * 2 * pairs), (other_ref, (1 - here) * 2 * pairs)):
        for pair in range(pairs):
            for tile in range(tiles):
                start = tile * LANES
                width = min(LANES, block - start)
                rows = [
                    raw_ref[tile, pl.ds(first + 2 * pair + part, windows, stride=2 * FREQS), :]
                    for part in (0, FREQS, 1, FREQS + 1)
                ]
                turned = jnp.concatenate(rows, axis=0).T
                out_ref[pair, start : start + width, :] = turned[:width].astype(jnp.bfloat16)


def merge_kernel(mine_ref, theirs_ref, *out_refs, total_windows):
    block, lanes = mine_ref.shape[1:]
    half = lanes // 2
    lane = lax.broadcasted_iota(jnp.int32, (block, lanes), 1)
    per_chunk = out_refs[0].shape[0]
    for pair in range(mine_ref.shape[0]):
        mine = mine_ref[pair].astype(jnp.float32)
        theirs = theirs_ref[pair].astype(jnp.float32)
        both = (
            jnp.where(lane < half, mine, pltpu.roll(theirs, half, 1)),
            jnp.where(lane < half, pltpu.roll(mine, half, 1), theirs),
        )
        for step, values in enumerate(both):
            power = jnp.sum(values * values, axis=1, keepdims=True)
            root = lax.rsqrt(power * (1.0 / total_windows) + 1e-06)
            bin_at = 2 * pair + step
            out_refs[bin_at // per_chunk][bin_at % per_chunk] = (values * root).astype(jnp.bfloat16)


def band_kernel(
    even_ref, own_ref, *refs, total_windows
):
    pieces = refs[: 2 * HOPS]
    mask_ref, real_ref, imag_ref, right_ref, left_ref = (*refs[2 * HOPS : 2 * HOPS + 1], *refs[-4:])
    block, depth = own_ref.shape[1:]
    reach = HOPS * block
    right_ref[:block] = own_ref[0]
    is_even = even_ref[0] == 1

    @pl.when(is_even)
    def _():
        for hop in range(HOPS):
            right_ref[(hop + 1) * block : (hop + 2) * block] = pieces[2 * hop][0]

    @pl.when(jnp.logical_not(is_even))
    def _():
        for hop in range(HOPS):
            right_ref[(hop + 1) * block : (hop + 2) * block] = pieces[2 * hop + 1][0]

    wide = own_ref[0].astype(jnp.float32) * (1.0 / math.sqrt(total_windows))
    part = depth // 4
    lane = lax.broadcasted_iota(jnp.int32, (block, depth), 1)
    turned = jnp.where(
        (lane // part) % 2 == 0, pltpu.roll(wide, depth - part, 1), -pltpu.roll(wide, part, 1)
    )
    for group in range(block // ROWS):
        at = slice(group * ROWS, (group + 1) * ROWS)
        left_ref[2 * group * ROWS : (2 * group + 1) * ROWS] = wide[at].astype(jnp.bfloat16)
        left_ref[(2 * group + 1) * ROWS : (2 * group + 2) * ROWS] = turned[at].astype(jnp.bfloat16)
    lane_of = lax.broadcasted_iota(jnp.int32, (ROWS, LANES), 1)
    row_of = lax.broadcasted_iota(jnp.int32, (ROWS, LANES), 0)
    out_tiles = -(-reach // LANES)
    for group in range(block // ROWS):
        first = group * ROWS
        base = (first + 1) // LANES
        shift = first + 1 - base * LANES + row_of
        tiles = (first + ROWS - 1 + reach) // LANES - base + 1
        products = lax.dot_general(
            left_ref[2 * first : 2 * first + 2 * ROWS],
            right_ref[base * LANES : (base + tiles) * LANES],
            (((1,), (1,)), ((), ())),
            preferred_element_type=jnp.float32,
        )
        keep = lane_of >= shift
        source = (lane_of + shift) % LANES
        for out_at, out_ref in enumerate((real_ref, imag_ref)):
            rows = products[out_at * ROWS : (out_at + 1) * ROWS]
            for tile in range(out_tiles):
                start = tile * LANES
                width = min(LANES, reach - start)
                values = rows[:, start : start + LANES]
                if tile + 1 < tiles:
                    values = jnp.where(keep, values, rows[:, start + LANES : start + 2 * LANES])
                moved = jnp.take_along_axis(values, source, axis=1, mode="promise_in_bounds")
                moved = moved.astype(jnp.bfloat16)
                if start + LANES > block:
                    moved = moved * mask_ref[first : first + ROWS, start : start + LANES]
                out_ref[0, first : first + ROWS, start : start + width] = moved[:, :width]


def band(even, own, pieces, mask, so_far, chunk, bins_here, total_windows):
    per_chunk, block, depth = own.shape
    out = jax.ShapeDtypeStruct((bins_here, block, HOPS * block), jnp.bfloat16)
    out_spec = pl.BlockSpec(
        (1, block, HOPS * block), lambda i, even: (chunk * per_chunk + i, 0, 0)
    )
    one = (1, block, depth)
    in_specs = [pl.BlockSpec(one, lambda i, even: (i, 0, 0))]
    operands = [even, own]
    for for_even, for_odd in pieces:
        in_specs.append(pl.BlockSpec(one, lambda i, even: (i * even[0], 0, 0)))
        in_specs.append(pl.BlockSpec(one, lambda i, even: (i * (1 - even[0]), 0, 0)))
        operands += [for_even, for_odd]
    in_specs.append(pl.BlockSpec(mask.shape, lambda i, even: (0, 0)))
    operands.append(mask)
    aliases = {}
    if so_far is not None:
        aliases = {len(operands): 0, len(operands) + 1: 1}
        operands += list(so_far)
        in_specs += [pl.BlockSpec(memory_space=pl.ANY)] * 2
    return pl.pallas_call(
        functools.partial(band_kernel, total_windows=total_windows),
        grid_spec=pltpu.PrefetchScalarGridSpec(
            num_scalar_prefetch=1,
            grid=(per_chunk,),
            in_specs=in_specs,
            out_specs=[out_spec, out_spec],
            scratch_shapes=[
                pltpu.VMEM(((HOPS + 1) * block, depth), jnp.bfloat16),
                pltpu.VMEM((2 * block, depth), jnp.bfloat16),
            ],
        ),
        out_shape=[out, out],
        input_output_aliases=aliases,
        cost_estimate=pl.CostEstimate(
            flops=per_chunk * 4 * block * (HOPS + 1) * block * depth,
            bytes_accessed=per_chunk * 4 * block * HOPS * block * 2,
            transcendentals=0,
        ),
        compiler_params=pltpu.CompilerParams(vmem_limit_bytes=24 << 20),
    )(*operands)


def body(samples, counts, reach_limit):
    windows_here, block, length = samples.shape
    tm_size = lax.axis_size("tm")
    fiber_size = lax.axis_size("fiber")
    total_windows = windows_here * tm_size
    bins_here = FREQS // tm_size
    per_chunk = bins_here // CHUNKS
    lanes = 4 * windows_here
    here = lax.axis_index("tm").astype(jnp.int32)
    is_even = lax.axis_index("fiber") % 2 == 0
    even = is_even.astype(jnp.int32)[None]

    pair_shape = jax.ShapeDtypeStruct((bins_here // 2, block, lanes), jnp.bfloat16)
    mine, other = pl.pallas_call(
        spectra_kernel,
        in_specs=[
            pl.BlockSpec(memory_space=pltpu.SMEM),
            pl.BlockSpec(memory_space=pltpu.VMEM),
            pl.BlockSpec(memory_space=pltpu.VMEM),
        ],
        out_specs=[pl.BlockSpec(memory_space=pltpu.VMEM)] * 2,
        out_shape=[pair_shape, pair_shape],
        scratch_shapes=[
            pltpu.VMEM((-(-block // LANES), windows_here * 2 * FREQS, LANES), jnp.float32)
        ],
        compiler_params=pltpu.CompilerParams(vmem_limit_bytes=32 << 20),
    )(
        jnp.stack([here, counts[0]]),
        samples,
        jnp.asarray(make_table(length, FREQS, FIRST_BIN)),
    )
    theirs = lax.ppermute(other, "tm", [(0, 1), (1, 0)])
    chunk_shape = jax.ShapeDtypeStruct((per_chunk, block, lanes), jnp.bfloat16)
    own = pl.pallas_call(
        functools.partial(merge_kernel, total_windows=total_windows),
        in_specs=[pl.BlockSpec(memory_space=pltpu.VMEM)] * 2,
        out_specs=[pl.BlockSpec(memory_space=pltpu.VMEM)] * CHUNKS,
        out_shape=[chunk_shape] * CHUNKS,
        compiler_params=pltpu.CompilerParams(vmem_limit_bytes=32 << 20),
    )(mine, theirs)

    down = [(i, i - 2) for i in range(2, fiber_size)]
    to_even = [(i, i - 1) for i in range(1, fiber_size, 2)]
    to_odd = [(i - 1, i) for i in range(1, fiber_size, 2)]

    def pick(for_even, for_odd):
        return jnp.where(is_even, for_even, for_odd)

    def move_down(for_even, for_odd):
        return lax.ppermute(pick(for_even, for_odd), "fiber", down)

    def cross(for_even, for_odd):
        return lax.ppermute(pick(for_even, for_odd), "fiber", to_even + to_odd)

    z, y = {}, {}
    z[0] = move_down(own[0], own[2])
    y[0] = lax.ppermute(own[0], "fiber", to_even)
    z[1] = move_down(own[1], own[3])
    y[1] = cross(z[0], own[1])
    z[2] = move_down(own[2], y[1])
    y[2] = cross(z[1], own[2])
    z[3] = move_down(own[3], y[2])
    y[3] = cross(z[2], own[3])
    z[4] = move_down(y[0], y[3])
    y[4] = cross(z[3], z[0])
    z[5] = move_down(y[1], y[4])
    y[5] = cross(z[4], z[1])
    y[6] = lax.ppermute(z[5], "fiber", to_odd)
    blocks = {
        0: ((y[0], y[1]), (z[0], y[5]), (z[4], z[2])),
        1: ((y[1], y[2]), (z[1], y[6]), (z[5], z[3])),
        2: ((y[2], y[3]), (z[2], z[0]), (y[4], z[4])),
        3: ((y[3], y[4]), (z[3], z[1]), (y[5], z[5])),
    }

    offsets = jnp.arange(1, -(-HOPS * block // LANES) * LANES + 1, dtype=jnp.int32)
    mask = (offsets[None, :] <= reach_limit[:, None]).astype(jnp.bfloat16)
    outs = None
    for chunk in (2, 0, 3, 1):
        outs = band(even, own[chunk], blocks[chunk], mask, outs, chunk, bins_here, total_windows)
    return tuple(outs)


def solution(mesh):
    placed = (P("tm", ("grp", "fiber"), None), P(("grp", "fiber")), P(("grp", "fiber")))
    return jax.shard_map(
        body,
        mesh=mesh,
        in_specs=placed,
        out_specs=(P("tm", ("grp", "fiber"), None), P("tm", ("grp", "fiber"), None)),
        check_vma=False,
    )
```

```python
import functools
import math

import jax
import jax.numpy as jnp
import ml_dtypes
import numpy as np
from jax import lax
from jax.experimental import pallas as pl
from jax.experimental.pallas import tpu as pltpu
from jax.sharding import PartitionSpec as P

FREQS = 32
FIRST_BIN = 8
LANES = 128
HOPS = 3
ROWS = 64
CHUNKS = 4
AT_ONCE = 8
VMEM = 60 << 20


def make_table(length, bins, first_bin):
    steps_index = np.arange(length, dtype=np.int32)
    bin_index = np.arange(bins, dtype=np.int32) + first_bin
    products = bin_index[:, None] * steps_index[None, :] % length
    phases = (2.0 * math.pi * products / length).astype(np.float32)
    taper = 0.5 - 0.5 * np.cos((2.0 * math.pi * steps_index / length).astype(np.float32))
    taper = taper.astype(np.float32)
    cosines = taper[None, :] * np.cos(phases)
    sines = -taper[None, :] * np.sin(phases)
    return np.concatenate([cosines, sines], axis=0).astype(ml_dtypes.bfloat16)


def spectra_kernel(place_ref, samples_ref, table_ref, mine_ref, other_ref, raw_ref):
    at_once, block, _ = samples_ref.shape
    step = pl.program_id(0)
    pairs = mine_ref.shape[0]
    here = place_ref[0]
    tiles = raw_ref.shape[0]
    channel = lax.broadcasted_iota(jnp.int32, (1, block), 1)
    active = (channel < place_ref[1]).astype(jnp.float32)
    for w in range(at_once):
        raw = lax.dot_general(
            table_ref[...], samples_ref[w], (((1,), (1,)), ((), ())),
            preferred_element_type=jnp.float32,
        )
        level = jnp.sum(raw * raw, axis=0, keepdims=True) * (1.0 / FREQS)
        white = raw * (lax.rsqrt(level + 1e-06) * active)
        for tile in range(tiles):
            start = tile * LANES
            width = min(LANES, block - start)
            rows = pl.ds(pl.multiple_of((step * at_once + w) * 2 * FREQS, 2 * FREQS), 2 * FREQS)
            raw_ref[tile, rows, :width] = white[:, start : start + width]

    @pl.when(step == pl.num_programs(0) - 1)
    def _():
        windows = raw_ref.shape[1] // (2 * FREQS)
        for out_ref, first in ((mine_ref, here * 2 * pairs), (other_ref, (1 - here) * 2 * pairs)):
            for pair in range(pairs):
                for tile in range(tiles):
                    start = tile * LANES
                    width = min(LANES, block - start)
                    rows = [
                        raw_ref[tile, pl.ds(first + 2 * pair + part, windows, stride=2 * FREQS), :]
                        for part in (0, FREQS, 1, FREQS + 1)
                    ]
                    turned = jnp.concatenate(rows, axis=0).T
                    out_ref[pair, start : start + width, :] = turned[:width].astype(jnp.bfloat16)


def merge_kernel(mine_ref, theirs_ref, *out_refs, total_windows):
    block, lanes = mine_ref.shape[1:]
    half = lanes // 2
    lane = lax.broadcasted_iota(jnp.int32, (block, lanes), 1)
    per_chunk = out_refs[0].shape[0]
    for pair in range(mine_ref.shape[0]):
        mine = mine_ref[pair].astype(jnp.float32)
        theirs = theirs_ref[pair].astype(jnp.float32)
        both = (
            jnp.where(lane < half, mine, pltpu.roll(theirs, half, 1)),
            jnp.where(lane < half, pltpu.roll(mine, half, 1), theirs),
        )
        for step, values in enumerate(both):
            power = jnp.sum(values * values, axis=1, keepdims=True)
            root = lax.rsqrt(power * (1.0 / total_windows) + 1e-06)
            bin_at = 2 * pair + step
            out_refs[bin_at // per_chunk][bin_at % per_chunk] = (values * root).astype(jnp.bfloat16)


def band_kernel(
    even_ref, own_ref, *refs, total_windows
):
    pieces = refs[: 2 * HOPS]
    mask_ref, real_ref, imag_ref, right_ref, left_ref = (*refs[2 * HOPS : 2 * HOPS + 1], *refs[-4:])
    block, depth = own_ref.shape[1:]
    reach = HOPS * block
    right_ref[:block] = own_ref[0]
    is_even = even_ref[0] == 1

    @pl.when(is_even)
    def _():
        for hop in range(HOPS):
            right_ref[(hop + 1) * block : (hop + 2) * block] = pieces[2 * hop][0]

    @pl.when(jnp.logical_not(is_even))
    def _():
        for hop in range(HOPS):
            right_ref[(hop + 1) * block : (hop + 2) * block] = pieces[2 * hop + 1][0]

    wide = own_ref[0].astype(jnp.float32) * (1.0 / math.sqrt(total_windows))
    part = depth // 4
    lane = lax.broadcasted_iota(jnp.int32, (block, depth), 1)
    turned = jnp.where(
        (lane // part) % 2 == 0, pltpu.roll(wide, depth - part, 1), -pltpu.roll(wide, part, 1)
    )
    for group in range(block // ROWS):
        at = slice(group * ROWS, (group + 1) * ROWS)
        left_ref[2 * group * ROWS : (2 * group + 1) * ROWS] = wide[at].astype(jnp.bfloat16)
        left_ref[(2 * group + 1) * ROWS : (2 * group + 2) * ROWS] = turned[at].astype(jnp.bfloat16)
    lane_of = lax.broadcasted_iota(jnp.int32, (ROWS, LANES), 1)
    row_of = lax.broadcasted_iota(jnp.int32, (ROWS, LANES), 0)
    out_tiles = -(-reach // LANES)
    for group in range(block // ROWS):
        first = group * ROWS
        base = (first + 1) // LANES
        shift = first + 1 - base * LANES + row_of
        tiles = (first + ROWS - 1 + reach) // LANES - base + 1
        products = lax.dot_general(
            left_ref[2 * first : 2 * first + 2 * ROWS],
            right_ref[base * LANES : (base + tiles) * LANES],
            (((1,), (1,)), ((), ())),
            preferred_element_type=jnp.float32,
        )
        keep = lane_of >= shift
        source = (lane_of + shift) % LANES
        for out_at, out_ref in enumerate((real_ref, imag_ref)):
            rows = products[out_at * ROWS : (out_at + 1) * ROWS]
            for tile in range(out_tiles):
                start = tile * LANES
                width = min(LANES, reach - start)
                values = rows[:, start : start + LANES]
                if tile + 1 < tiles:
                    values = jnp.where(keep, values, rows[:, start + LANES : start + 2 * LANES])
                moved = jnp.take_along_axis(values, source, axis=1, mode="promise_in_bounds")
                moved = moved.astype(jnp.bfloat16)
                if start + LANES > block:
                    moved = moved * mask_ref[first : first + ROWS, start : start + LANES]
                out_ref[0, first : first + ROWS, start : start + width] = moved[:, :width]


def band(even, own, pieces, mask, so_far, chunk, bins_here, total_windows):
    per_chunk, block, depth = own.shape
    out = jax.ShapeDtypeStruct((bins_here, block, HOPS * block), jnp.bfloat16)
    out_spec = pl.BlockSpec(
        (1, block, HOPS * block), lambda i, even: (chunk * per_chunk + i, 0, 0)
    )
    one = (1, block, depth)
    in_specs = [pl.BlockSpec(one, lambda i, even: (i, 0, 0))]
    operands = [even, own]
    for for_even, for_odd in pieces:
        in_specs.append(pl.BlockSpec(one, lambda i, even: (i * even[0], 0, 0)))
        in_specs.append(pl.BlockSpec(one, lambda i, even: (i * (1 - even[0]), 0, 0)))
        operands += [for_even, for_odd]
    in_specs.append(pl.BlockSpec(mask.shape, lambda i, even: (0, 0)))
    operands.append(mask)
    aliases = {}
    if so_far is not None:
        aliases = {len(operands): 0, len(operands) + 1: 1}
        operands += list(so_far)
        in_specs += [pl.BlockSpec(memory_space=pl.ANY)] * 2
    return pl.pallas_call(
        functools.partial(band_kernel, total_windows=total_windows),
        grid_spec=pltpu.PrefetchScalarGridSpec(
            num_scalar_prefetch=1,
            grid=(per_chunk,),
            in_specs=in_specs,
            out_specs=[out_spec, out_spec],
            scratch_shapes=[
                pltpu.VMEM(((HOPS + 1) * block, depth), jnp.bfloat16),
                pltpu.VMEM((2 * block, depth), jnp.bfloat16),
            ],
        ),
        out_shape=[out, out],
        input_output_aliases=aliases,
        cost_estimate=pl.CostEstimate(
            flops=per_chunk * 4 * block * (HOPS + 1) * block * depth,
            bytes_accessed=per_chunk * 4 * block * HOPS * block * 2,
            transcendentals=0,
        ),
        compiler_params=pltpu.CompilerParams(vmem_limit_bytes=VMEM),
    )(*operands)


def body(samples, counts, reach_limit):
    windows_here, block, length = samples.shape
    tm_size = lax.axis_size("tm")
    fiber_size = lax.axis_size("fiber")
    total_windows = windows_here * tm_size
    bins_here = FREQS // tm_size
    per_chunk = bins_here // CHUNKS
    lanes = 4 * windows_here
    here = lax.axis_index("tm").astype(jnp.int32)
    is_even = lax.axis_index("fiber") % 2 == 0
    even = is_even.astype(jnp.int32)[None]

    pair_shape = jax.ShapeDtypeStruct((bins_here // 2, block, lanes), jnp.bfloat16)
    mine, other = pl.pallas_call(
        spectra_kernel,
        grid=(windows_here // AT_ONCE,),
        in_specs=[
            pl.BlockSpec(memory_space=pltpu.SMEM),
            pl.BlockSpec((AT_ONCE, block, length), lambda i: (i, 0, 0)),
            pl.BlockSpec((2 * FREQS, length), lambda i: (0, 0)),
        ],
        out_specs=[pl.BlockSpec(pair_shape.shape, lambda i: (0, 0, 0))] * 2,
        out_shape=[pair_shape, pair_shape],
        scratch_shapes=[
            pltpu.VMEM((-(-block // LANES), windows_here * 2 * FREQS, LANES), jnp.float32)
        ],
        compiler_params=pltpu.CompilerParams(vmem_limit_bytes=VMEM),
    )(
        jnp.stack([here, counts[0]]),
        samples,
        jnp.asarray(make_table(length, FREQS, FIRST_BIN)),
    )
    theirs = lax.ppermute(other, "tm", [(0, 1), (1, 0)])
    chunk_shape = jax.ShapeDtypeStruct((per_chunk, block, lanes), jnp.bfloat16)
    own = pl.pallas_call(
        functools.partial(merge_kernel, total_windows=total_windows),
        in_specs=[pl.BlockSpec(memory_space=pltpu.VMEM)] * 2,
        out_specs=[pl.BlockSpec(memory_space=pltpu.VMEM)] * CHUNKS,
        out_shape=[chunk_shape] * CHUNKS,
        compiler_params=pltpu.CompilerParams(vmem_limit_bytes=32 << 20),
    )(mine, theirs)

    down = [(i, i - 2) for i in range(2, fiber_size)]
    to_even = [(i, i - 1) for i in range(1, fiber_size, 2)]
    to_odd = [(i - 1, i) for i in range(1, fiber_size, 2)]

    def pick(for_even, for_odd):
        even_one, for_even, for_odd = lax.optimization_barrier((is_even, for_even, for_odd))
        return lax.optimization_barrier(jnp.where(even_one, for_even, for_odd))

    def move_down(for_even, for_odd):
        return lax.ppermute(pick(for_even, for_odd), "fiber", down)

    def cross(for_even, for_odd):
        return lax.ppermute(pick(for_even, for_odd), "fiber", to_even + to_odd)

    z, y = {}, {}
    z[0] = move_down(own[0], own[2])
    y[0] = lax.ppermute(own[0], "fiber", to_even)
    z[1] = move_down(own[1], own[3])
    z[0], y[0] = lax.optimization_barrier((z[0], y[0]))
    y[1] = cross(z[0], own[1])
    z[2] = move_down(own[2], y[1])
    y[2] = cross(z[1], own[2])
    z[3] = move_down(own[3], y[2])
    y[3] = cross(z[2], own[3])
    z[4] = move_down(y[0], y[3])
    y[4] = cross(z[3], z[0])
    z[5] = move_down(y[1], y[4])
    y[5] = cross(z[4], z[1])
    offsets = jnp.arange(1, -(-HOPS * block // LANES) * LANES + 1, dtype=jnp.int32)
    mask = (offsets[None, :] <= reach_limit[:, None]).astype(jnp.bfloat16)

    def work(outs, chunk, *pieces):
        return band(even, own[chunk], pieces, mask, outs, chunk, bins_here, total_windows)

    outs = work(None, 2, (y[2], y[3]), (z[2], z[0]), (y[4], z[4]))
    z[5], *outs = lax.optimization_barrier((z[5], *outs))
    y[6] = lax.ppermute(z[5], "fiber", to_odd)
    outs = work(outs, 0, (y[0], y[1]), (z[0], y[5]), (z[4], z[2]))
    outs = work(outs, 3, (y[3], y[4]), (z[3], z[1]), (y[5], z[5]))
    outs = work(outs, 1, (y[1], y[2]), (z[1], y[6]), (z[5], z[3]))
    return tuple(outs)


def solution(mesh):
    placed = (P("tm", ("grp", "fiber"), None), P(("grp", "fiber")), P(("grp", "fiber")))
    return jax.shard_map(
        body,
        mesh=mesh,
        in_specs=placed,
        out_specs=(P("tm", ("grp", "fiber"), None), P("tm", ("grp", "fiber"), None)),
        check_vma=False,
    )
```

```python
import functools
import math

import jax
import jax.numpy as jnp
import ml_dtypes
import numpy as np
from jax import lax
from jax.experimental import pallas as pl
from jax.experimental.pallas import tpu as pltpu
from jax.sharding import PartitionSpec as P

FREQS = 32
FIRST_BIN = 8
LANES = 128
HOPS = 3
ROWS = 64
CHUNKS = 4
VMEM = 16 << 20


def make_table(length, bins, first_bin):
    steps_index = np.arange(length, dtype=np.int32)
    bin_index = np.arange(bins, dtype=np.int32) + first_bin
    products = bin_index[:, None] * steps_index[None, :] % length
    phases = (2.0 * math.pi * products / length).astype(np.float32)
    taper = 0.5 - 0.5 * np.cos((2.0 * math.pi * steps_index / length).astype(np.float32))
    taper = taper.astype(np.float32)
    cosines = taper[None, :] * np.cos(phases)
    sines = -taper[None, :] * np.sin(phases)
    return np.concatenate([cosines, sines], axis=0).astype(ml_dtypes.bfloat16)


def spectra_kernel(place_ref, samples_ref, table_ref, mine_ref, other_ref, raw_ref):
    windows, block, _ = samples_ref.shape
    pairs = mine_ref.shape[0]
    here = place_ref[0]
    tiles = raw_ref.shape[0]
    channel = lax.broadcasted_iota(jnp.int32, (1, block), 1)
    active = (channel < place_ref[1]).astype(jnp.float32)
    for w in range(windows):
        raw = lax.dot_general(
            table_ref[...], samples_ref[w], (((1,), (1,)), ((), ())),
            preferred_element_type=jnp.float32,
        )
        level = jnp.sum(raw * raw, axis=0, keepdims=True) * (1.0 / FREQS)
        white = raw * (lax.rsqrt(level + 1e-06) * active)
        for tile in range(tiles):
            start = tile * LANES
            width = min(LANES, block - start)
            raw_ref[tile, w * 2 * FREQS : (w + 1) * 2 * FREQS, :width] = white[:, start : start + width]
    for out_ref, first in ((mine_ref, here * 2 * pairs), (other_ref, (1 - here) * 2 * pairs)):
        for pair in range(pairs):
            for tile in range(tiles):
                start = tile * LANES
                width = min(LANES, block - start)
                rows = [
                    raw_ref[tile, pl.ds(first + 2 * pair + part, windows, stride=2 * FREQS), :]
                    for part in (0, FREQS, 1, FREQS + 1)
                ]
                turned = jnp.concatenate(rows, axis=0).T
                out_ref[pair, start : start + width, :] = turned[:width].astype(jnp.bfloat16)


def merge_kernel(mine_ref, theirs_ref, *out_refs, total_windows):
    block, lanes = mine_ref.shape[1:]
    half = lanes // 2
    lane = lax.broadcasted_iota(jnp.int32, (block, lanes), 1)
    per_chunk = out_refs[0].shape[0]
    for pair in range(mine_ref.shape[0]):
        mine = mine_ref[pair].astype(jnp.float32)
        theirs = theirs_ref[pair].astype(jnp.float32)
        both = (
            jnp.where(lane < half, mine, pltpu.roll(theirs, half, 1)),
            jnp.where(lane < half, pltpu.roll(mine, half, 1), theirs),
        )
        for step, values in enumerate(both):
            power = jnp.sum(values * values, axis=1, keepdims=True)
            root = lax.rsqrt(power * (1.0 / total_windows) + 1e-06)
            bin_at = 2 * pair + step
            out_refs[bin_at // per_chunk][bin_at % per_chunk] = (values * root).astype(jnp.bfloat16)


def band_kernel(even_ref, own_ref, *refs, hops, first_tile, total_windows):
    at = pl.program_id(0)
    far = [hop for hop in hops if hop]
    pieces = refs[: 2 * len(far)]
    mask_ref, real_ref, imag_ref = (refs[2 * len(far)], *refs[-4:-2])
    right_ref, left_ref = refs[-2:]
    _, block, depth = own_ref.shape
    reach = min(HOPS * block - first_tile * LANES, real_ref.shape[2])
    is_even = even_ref[0] == 1
    origin = hops[0] * block
    if hops[0] == 0:
        right_ref[:block] = own_ref[at]

    def gather(parity):
        for place, hop in enumerate(far):
            start = hop * block - origin
            right_ref[start : start + block] = pieces[2 * place + parity][at]

    filled = len(hops) * block
    if right_ref.shape[0] > filled:
        right_ref[filled:] = jnp.zeros((right_ref.shape[0] - filled, depth), jnp.bfloat16)
    pl.when(is_even)(lambda: gather(0))
    pl.when(jnp.logical_not(is_even))(lambda: gather(1))

    wide = own_ref[at].astype(jnp.float32) * (1.0 / math.sqrt(total_windows))
    part = depth // 4
    lane = lax.broadcasted_iota(jnp.int32, (block, depth), 1)
    turned = jnp.where(
        (lane // part) % 2 == 0, pltpu.roll(wide, depth - part, 1), -pltpu.roll(wide, part, 1)
    )
    for group in range(block // ROWS):
        rows = slice(group * ROWS, (group + 1) * ROWS)
        left_ref[2 * group * ROWS : (2 * group + 1) * ROWS] = wide[rows].astype(jnp.bfloat16)
        left_ref[(2 * group + 1) * ROWS : (2 * group + 2) * ROWS] = turned[rows].astype(jnp.bfloat16)
    lane_of = lax.broadcasted_iota(jnp.int32, (ROWS, LANES), 1)
    row_of = lax.broadcasted_iota(jnp.int32, (ROWS, LANES), 0)
    out_tiles = -(-reach // LANES)
    mask_from = 2 if first_tile == 0 else 0
    for group in range(block // ROWS):
        first = group * ROWS
        begin = first + 1 + first_tile * LANES - origin
        base = begin // LANES
        shift = begin - base * LANES + row_of
        tiles = (begin + ROWS - 2 + reach) // LANES - base + 1
        products = lax.dot_general(
            left_ref[2 * first : 2 * first + 2 * ROWS],
            right_ref[base * LANES : (base + tiles) * LANES],
            (((1,), (1,)), ((), ())),
            preferred_element_type=jnp.float32,
        )
        keep = lane_of >= shift
        source = (lane_of + shift) % LANES
        for out_at, out_ref in enumerate((real_ref, imag_ref)):
            rows = products[out_at * ROWS : (out_at + 1) * ROWS]
            for tile in range(out_tiles):
                start = tile * LANES
                width = min(LANES, reach - start)
                values = rows[:, start : start + LANES]
                if tile + 1 < tiles:
                    values = jnp.where(keep, values, rows[:, start + LANES : start + 2 * LANES])
                moved = jnp.take_along_axis(values, source, axis=1, mode="promise_in_bounds")
                moved = moved.astype(jnp.bfloat16)
                if tile >= mask_from:
                    column = (tile - mask_from) * LANES
                    moved = moved * mask_ref[first : first + ROWS, column : column + LANES]
                out_ref[0, first : first + ROWS, start : start + width] = moved[:, :width]


def band(even, own, pieces, mask, so_far, chunk, bins_here, total_windows, far):
    per_chunk, block, depth = own.shape
    out = jax.ShapeDtypeStruct((bins_here, block, HOPS * block), jnp.bfloat16)
    near_width = 2 * block
    hops = (2, 3) if far else (0, 1, 2)
    out_spec = pl.BlockSpec(
        (1, block, near_width), lambda i: (chunk * per_chunk + i, 0, 1 if far else 0)
    )
    operands = [even, own]
    for piece in pieces:
        operands += piece
    operands.append(mask)
    in_specs = [pl.BlockSpec(memory_space=pltpu.SMEM)]
    in_specs += [pl.BlockSpec(memory_space=pltpu.VMEM)] * (len(operands) - 1)
    aliases = {}
    if so_far is not None:
        aliases = {len(operands): 0, len(operands) + 1: 1}
        operands += list(so_far)
        in_specs += [pl.BlockSpec(memory_space=pl.ANY)] * 2
    wide = block if far else near_width
    return pl.pallas_call(
        functools.partial(
            band_kernel,
            hops=hops,
            first_tile=near_width // LANES if far else 0,
            total_windows=total_windows,
        ),
        grid=(per_chunk,),
        in_specs=in_specs,
        out_specs=[out_spec, out_spec],
        scratch_shapes=[
            pltpu.VMEM((-(-len(hops) * block // LANES) * LANES, depth), jnp.bfloat16),
            pltpu.VMEM((2 * block, depth), jnp.bfloat16),
        ],
        out_shape=[out, out],
        input_output_aliases=aliases,
        cost_estimate=pl.CostEstimate(
            flops=per_chunk * 4 * block * wide * depth,
            bytes_accessed=per_chunk * 4 * block * wide,
            transcendentals=0,
        ),
        compiler_params=pltpu.CompilerParams(vmem_limit_bytes=VMEM),
    )(*operands)


def body(samples, counts, reach_limit):
    windows_here, block, length = samples.shape
    tm_size = lax.axis_size("tm")
    fiber_size = lax.axis_size("fiber")
    total_windows = windows_here * tm_size
    bins_here = FREQS // tm_size
    per_chunk = bins_here // CHUNKS
    lanes = 4 * windows_here
    here = lax.axis_index("tm").astype(jnp.int32)
    is_even = lax.axis_index("fiber") % 2 == 0
    even = is_even.astype(jnp.int32)[None]

    pair_shape = jax.ShapeDtypeStruct((bins_here // 2, block, lanes), jnp.bfloat16)
    mine, other = pl.pallas_call(
        spectra_kernel,
        in_specs=[
            pl.BlockSpec(memory_space=pltpu.SMEM),
            pl.BlockSpec(memory_space=pltpu.VMEM),
            pl.BlockSpec(memory_space=pltpu.VMEM),
        ],
        out_specs=[pl.BlockSpec(memory_space=pltpu.VMEM)] * 2,
        out_shape=[pair_shape, pair_shape],
        scratch_shapes=[
            pltpu.VMEM((-(-block // LANES), windows_here * 2 * FREQS, LANES), jnp.float32)
        ],
        compiler_params=pltpu.CompilerParams(vmem_limit_bytes=VMEM),
    )(
        jnp.stack([here, counts[0]]),
        samples,
        jnp.asarray(make_table(length, FREQS, FIRST_BIN)),
    )
    theirs = lax.ppermute(other, "tm", [(0, 1), (1, 0)])
    chunk_shape = jax.ShapeDtypeStruct((per_chunk, block, lanes), jnp.bfloat16)
    own = pl.pallas_call(
        functools.partial(merge_kernel, total_windows=total_windows),
        in_specs=[pl.BlockSpec(memory_space=pltpu.VMEM)] * 2,
        out_specs=[pl.BlockSpec(memory_space=pltpu.VMEM)] * CHUNKS,
        out_shape=[chunk_shape] * CHUNKS,
        compiler_params=pltpu.CompilerParams(vmem_limit_bytes=32 << 20),
    )(mine, theirs)

    down = [(i, i - 2) for i in range(2, fiber_size)]
    to_even = [(i, i - 1) for i in range(1, fiber_size, 2)]
    to_odd = [(i - 1, i) for i in range(1, fiber_size, 2)]

    def pick(for_even, for_odd):
        even_one, for_even, for_odd = lax.optimization_barrier((is_even, for_even, for_odd))
        return lax.optimization_barrier(jnp.where(even_one, for_even, for_odd))

    def move_down(for_even, for_odd):
        return lax.ppermute(pick(for_even, for_odd), "fiber", down)

    def cross(for_even, for_odd):
        return lax.ppermute(pick(for_even, for_odd), "fiber", to_even + to_odd)

    near = 2 * block
    offsets = jnp.arange(1, near + HOPS * LANES + 1, dtype=jnp.int32)
    mask = (offsets[None, :] <= reach_limit[:, None]).astype(jnp.bfloat16)
    masks = (mask[:, 2 * LANES : near], mask[:, near:])

    def work(outs, chunk, far, *pieces):
        return band(
            even, own[chunk], pieces, masks[far], outs, chunk, bins_here, total_windows, far
        )

    z, y = {}, {}
    z[0] = move_down(own[0], own[2])
    y[0] = lax.ppermute(own[0], "fiber", to_even)
    z[1] = move_down(own[1], own[3])
    z[0], y[0], *masks = lax.optimization_barrier((z[0], y[0], *masks))
    y[1] = cross(z[0], own[1])
    z[2] = move_down(own[2], y[1])
    y[2] = cross(z[1], own[2])
    z[3] = move_down(own[3], y[2])
    y[3] = cross(z[2], own[3])
    z[4] = move_down(y[0], y[3])
    y[4] = cross(z[3], z[0])
    outs = work(None, 2, 0, (y[2], y[3]), (z[2], z[0]))
    z[4], *outs = lax.optimization_barrier((z[4], *outs))
    z[5] = move_down(y[1], y[4])
    y[5] = cross(z[4], z[1])
    outs = work(outs, 3, 0, (y[3], y[4]), (z[3], z[1]))
    outs = work(outs, 2, 1, (z[2], z[0]), (y[4], z[4]))
    z[5], *outs = lax.optimization_barrier((z[5], *outs))
    y[6] = lax.ppermute(z[5], "fiber", to_odd)
    outs = work(outs, 3, 1, (z[3], z[1]), (y[5], z[5]))
    outs = work(outs, 0, 0, (y[0], y[1]), (z[0], y[5]))
    outs = work(outs, 0, 1, (z[0], y[5]), (z[4], z[2]))
    outs = work(outs, 1, 0, (y[1], y[2]), (z[1], y[6]))
    outs = work(outs, 1, 1, (z[1], y[6]), (z[5], z[3]))
    return tuple(outs)


def solution(mesh):
    placed = (P("tm", ("grp", "fiber"), None), P(("grp", "fiber")), P(("grp", "fiber")))
    return jax.shard_map(
        body,
        mesh=mesh,
        in_specs=placed,
        out_specs=(P("tm", ("grp", "fiber"), None), P("tm", ("grp", "fiber"), None)),
        check_vma=False,
    )
```

```python
import functools
import math

import jax
import jax.numpy as jnp
import ml_dtypes
import numpy as np
from jax import lax
from jax.experimental import pallas as pl
from jax.experimental.pallas import tpu as pltpu
from jax.sharding import PartitionSpec as P

FREQS = 32
FIRST_BIN = 8
LANES = 128
HOPS = 3
ROWS = 64
CHUNKS = 4
VMEM = 16 << 20


def make_table(length, bins, first_bin):
    steps_index = np.arange(length, dtype=np.int32)
    bin_index = np.arange(bins, dtype=np.int32) + first_bin
    products = bin_index[:, None] * steps_index[None, :] % length
    phases = (2.0 * math.pi * products / length).astype(np.float32)
    taper = 0.5 - 0.5 * np.cos((2.0 * math.pi * steps_index / length).astype(np.float32))
    taper = taper.astype(np.float32)
    cosines = taper[None, :] * np.cos(phases)
    sines = -taper[None, :] * np.sin(phases)
    return np.concatenate([cosines, sines], axis=0).astype(ml_dtypes.bfloat16)


def spectra_kernel(place_ref, samples_ref, table_ref, mine_ref, other_ref, raw_ref):
    windows, block, _ = samples_ref.shape
    pairs = mine_ref.shape[0]
    here = place_ref[0]
    tiles = raw_ref.shape[0]
    channel = lax.broadcasted_iota(jnp.int32, (1, block), 1)
    active = (channel < place_ref[1]).astype(jnp.float32)
    for w in range(windows):
        raw = lax.dot_general(
            table_ref[...], samples_ref[w], (((1,), (1,)), ((), ())),
            preferred_element_type=jnp.float32,
        )
        level = jnp.sum(raw * raw, axis=0, keepdims=True) * (1.0 / FREQS)
        white = raw * (lax.rsqrt(level + 1e-06) * active)
        for tile in range(tiles):
            start = tile * LANES
            width = min(LANES, block - start)
            raw_ref[tile, w * 2 * FREQS : (w + 1) * 2 * FREQS, :width] = white[:, start : start + width]
    for out_ref, first in ((mine_ref, here * 2 * pairs), (other_ref, (1 - here) * 2 * pairs)):
        for pair in range(pairs):
            for tile in range(tiles):
                start = tile * LANES
                width = min(LANES, block - start)
                rows = [
                    raw_ref[tile, pl.ds(first + 2 * pair + part, windows, stride=2 * FREQS), :]
                    for part in (0, FREQS, 1, FREQS + 1)
                ]
                turned = jnp.concatenate(rows, axis=0).T
                out_ref[pair, start : start + width, :] = turned[:width].astype(jnp.bfloat16)


def merge_kernel(mine_ref, theirs_ref, *out_refs, total_windows):
    block, lanes = mine_ref.shape[1:]
    chunk_refs, half_refs, left_refs = out_refs[:CHUNKS], out_refs[CHUNKS:-CHUNKS], out_refs[-CHUNKS:]
    half = lanes // 2
    part = lanes // 4
    lane = lax.broadcasted_iota(jnp.int32, (block, lanes), 1)
    is_real = (lane // part) % 2 == 0
    per_chunk = chunk_refs[0].shape[0]
    per_half = half_refs[0].shape[0]
    for pair in range(mine_ref.shape[0]):
        mine = mine_ref[pair].astype(jnp.float32)
        theirs = theirs_ref[pair].astype(jnp.float32)
        both = (
            jnp.where(lane < half, mine, pltpu.roll(theirs, half, 1)),
            jnp.where(lane < half, pltpu.roll(mine, half, 1), theirs),
        )
        for step, values in enumerate(both):
            power = jnp.sum(values * values, axis=1, keepdims=True)
            root = lax.rsqrt(power * (1.0 / total_windows) + 1e-06)
            bin_at = 2 * pair + step
            scaled = values * root
            rounded = scaled.astype(jnp.bfloat16)
            chunk_refs[bin_at // per_chunk][bin_at % per_chunk] = rounded
            half_refs[bin_at // per_half][bin_at % per_half] = rounded
            straight = scaled * (1.0 / math.sqrt(total_windows))
            turned = jnp.where(
                is_real, pltpu.roll(straight, lanes - part, 1), -pltpu.roll(straight, part, 1)
            )
            left_ref = left_refs[bin_at // per_chunk]
            for group in range(block // ROWS):
                rows = slice(group * ROWS, (group + 1) * ROWS)
                for place, operand in enumerate((straight, turned)):
                    start = (2 * group + place) * ROWS
                    left_ref[bin_at % per_chunk, start : start + ROWS] = operand[rows].astype(
                        jnp.bfloat16
                    )


def band_kernel(*refs, chunks, sources, hops, first_tile):
    step = pl.program_id(0)
    mask_ref, real_ref, imag_ref, right_ref, left_ref = (refs[0], *refs[-4:])
    _, block, width = real_ref.shape
    depth = right_ref.shape[1]
    reach = min(HOPS * block - first_tile * LANES, width)
    origin = hops[0] * block
    filled = len(hops) * block
    per_chunk = pl.num_programs(0) // chunks
    parity = lax.rem(lax.axis_index("fiber"), 2)
    if right_ref.shape[0] > filled:
        right_ref[filled:] = jnp.zeros((right_ref.shape[0] - filled, depth), jnp.bfloat16)

    def gather(at, places, odd):
        for hop, place in zip(hops, places):
            operand, first_bin = place[odd]
            start = hop * block - origin
            right_ref[start : start + block] = refs[operand][first_bin + at]

    for chunk, (left, places) in enumerate(sources):
        at = step - chunk * per_chunk
        here = jnp.logical_and(at >= 0, at < per_chunk)

        @pl.when(jnp.logical_and(here, parity == 0))
        def _(at=at, places=places):
            gather(at, places, 0)

        @pl.when(jnp.logical_and(here, parity == 1))
        def _(at=at, places=places):
            gather(at, places, 1)

        if chunks > 1:
            @pl.when(here)
            def _(at=at, left=left):
                left_ref[...] = refs[left][at]

    def left_rows(start, size):
        if chunks > 1:
            return left_ref[start : start + size]
        return refs[sources[0][0]][step, start : start + size]

    lane_of = lax.broadcasted_iota(jnp.int32, (ROWS, LANES), 1)
    row_of = lax.broadcasted_iota(jnp.int32, (ROWS, LANES), 0)
    out_tiles = -(-reach // LANES)
    mask_from = 2 if first_tile == 0 else 0
    for group in range(block // ROWS):
        first = group * ROWS
        begin = first + 1 + first_tile * LANES - origin
        base = begin // LANES
        shift = begin - base * LANES + row_of
        tiles = (begin + ROWS - 2 + reach) // LANES - base + 1
        products = lax.dot_general(
            left_rows(2 * first, 2 * ROWS),
            right_ref[base * LANES : (base + tiles) * LANES],
            (((1,), (1,)), ((), ())),
            preferred_element_type=jnp.float32,
        )
        keep = lane_of >= shift
        source = (lane_of + shift) % LANES
        for out_at, out_ref in enumerate((real_ref, imag_ref)):
            rows = products[out_at * ROWS : (out_at + 1) * ROWS]
            for tile in range(out_tiles):
                start = tile * LANES
                wide = min(LANES, reach - start)
                values = rows[:, start : start + LANES]
                if tile + 1 < tiles:
                    values = jnp.where(keep, values, rows[:, start + LANES : start + 2 * LANES])
                moved = jnp.take_along_axis(values, source, axis=1, mode="promise_in_bounds")
                moved = moved.astype(jnp.bfloat16)
                if tile >= mask_from:
                    column = (tile - mask_from) * LANES
                    moved = moved * mask_ref[first : first + ROWS, column : column + LANES]
                out_ref[0, first : first + ROWS, start : start + wide] = moved[:, :wide]


def band(first_chunk, far, parts, mask, so_far, bins_here):
    per_chunk, _, depth = parts[0][0].shape
    block = mask.shape[0]
    chunks = len(parts)
    out = jax.ShapeDtypeStruct((bins_here, block, HOPS * block), jnp.bfloat16)
    near_width = 2 * block
    hops = (2, 3) if far else (0, 1, 2)
    first_bin = first_chunk * per_chunk
    out_spec = pl.BlockSpec((1, block, near_width), lambda i: (first_bin + i, 0, 1 if far else 0))
    operands = [mask]

    def index_of(array):
        for at, operand in enumerate(operands):
            if operand is array:
                return at
        operands.append(array)
        return len(operands) - 1

    sources = [
        (
            index_of(left),
            [tuple((index_of(array), offset) for array, offset in place) for place in places],
        )
        for left, places in parts
    ]
    in_specs = [pl.BlockSpec(memory_space=pltpu.VMEM)] * len(operands)
    aliases = {}
    if so_far is not None:
        aliases = {len(operands): 0, len(operands) + 1: 1}
        operands += list(so_far)
        in_specs += [pl.BlockSpec(memory_space=pl.ANY)] * 2
    wide = block if far else near_width
    return pl.pallas_call(
        functools.partial(
            band_kernel,
            chunks=chunks,
            sources=sources,
            hops=hops,
            first_tile=near_width // LANES if far else 0,
        ),
        grid=(chunks * per_chunk,),
        in_specs=in_specs,
        out_specs=[out_spec, out_spec],
        scratch_shapes=[
            pltpu.VMEM((-(-len(hops) * block // LANES) * LANES, depth), jnp.bfloat16),
            pltpu.VMEM((2 * block, depth), jnp.bfloat16),
        ],
        out_shape=[out, out],
        input_output_aliases=aliases,
        cost_estimate=pl.CostEstimate(
            flops=chunks * per_chunk * 4 * block * wide * depth,
            bytes_accessed=chunks * per_chunk * 4 * block * wide,
            transcendentals=0,
        ),
        compiler_params=pltpu.CompilerParams(vmem_limit_bytes=VMEM),
    )(*operands)


def body(samples, counts, reach_limit):
    windows_here, block, length = samples.shape
    tm_size = lax.axis_size("tm")
    fiber_size = lax.axis_size("fiber")
    total_windows = windows_here * tm_size
    bins_here = FREQS // tm_size
    per_chunk = bins_here // CHUNKS
    lanes = 4 * windows_here
    here = lax.axis_index("tm").astype(jnp.int32)
    is_even = lax.axis_index("fiber") % 2 == 0

    pair_shape = jax.ShapeDtypeStruct((bins_here // 2, block, lanes), jnp.bfloat16)
    mine, other = pl.pallas_call(
        spectra_kernel,
        in_specs=[
            pl.BlockSpec(memory_space=pltpu.SMEM),
            pl.BlockSpec(memory_space=pltpu.VMEM),
            pl.BlockSpec(memory_space=pltpu.VMEM),
        ],
        out_specs=[pl.BlockSpec(memory_space=pltpu.VMEM)] * 2,
        out_shape=[pair_shape, pair_shape],
        scratch_shapes=[
            pltpu.VMEM((-(-block // LANES), windows_here * 2 * FREQS, LANES), jnp.float32)
        ],
        compiler_params=pltpu.CompilerParams(vmem_limit_bytes=VMEM),
    )(
        jnp.stack([here, counts[0]]),
        samples,
        jnp.asarray(make_table(length, FREQS, FIRST_BIN)),
    )
    theirs = lax.ppermute(other, "tm", [(0, 1), (1, 0)])
    chunk_shape = jax.ShapeDtypeStruct((per_chunk, block, lanes), jnp.bfloat16)
    half_shape = jax.ShapeDtypeStruct((bins_here // 2, block, lanes), jnp.bfloat16)
    left_shape = jax.ShapeDtypeStruct((per_chunk, 2 * block, lanes), jnp.bfloat16)
    shapes = [chunk_shape] * CHUNKS + [half_shape] * 2 + [left_shape] * CHUNKS
    merged = pl.pallas_call(
        functools.partial(merge_kernel, total_windows=total_windows),
        in_specs=[pl.BlockSpec(memory_space=pltpu.VMEM)] * 2,
        out_specs=[pl.BlockSpec(memory_space=pltpu.VMEM)] * len(shapes),
        out_shape=shapes,
        compiler_params=pltpu.CompilerParams(vmem_limit_bytes=32 << 20),
    )(mine, theirs)
    own, halves, left = merged[:CHUNKS], merged[CHUNKS:-CHUNKS], merged[-CHUNKS:]

    down = [(i, i - 2) for i in range(2, fiber_size)]
    down_odd = [(i, i - 2) for i in range(3, fiber_size, 2)]
    to_even = [(i, i - 1) for i in range(1, fiber_size, 2)]
    to_odd = [(i - 1, i) for i in range(1, fiber_size, 2)]

    def pick(for_even, for_odd):
        even_one, for_even, for_odd = lax.optimization_barrier((is_even, for_even, for_odd))
        return lax.optimization_barrier(jnp.where(even_one, for_even, for_odd))

    def send(payload, route):
        return lax.ppermute(payload, "fiber", route)

    def after(payload, *others):
        return lax.optimization_barrier((payload, *others))

    near_reach = 2 * block
    offsets = jnp.arange(1, near_reach + HOPS * LANES + 1, dtype=jnp.int32)
    mask = (offsets[None, :] <= reach_limit[:, None]).astype(jnp.bfloat16)
    masks = (mask[:, 2 * LANES : near_reach], mask[:, near_reach:])

    def near(outs, chunk):
        first = chunk % 2 * per_chunk
        places = [
            ((own[chunk], 0), (own[chunk], 0)),
            ((ahead[chunk // 2], first), (up[chunk], 0)),
            ((z[chunk], 0), (z[chunk], 0)),
        ]
        return band(chunk, 0, [(left[chunk], places)], masks[0], outs, bins_here)

    def far(outs, first_chunk, count):
        last = [(z[5], up[4]), (back[1], z[4]), (back[2], z[5]), (back[3], z[6])]
        parts = []
        for chunk in range(first_chunk, first_chunk + count):
            places = [
                ((z[chunk], 0), (z[chunk], 0)),
                ((last[chunk][0], 0), (last[chunk][1], 0)),
            ]
            parts.append((left[chunk], places))
        return band(first_chunk, 1, parts, masks[1], outs, bins_here)

    z, up, ahead, back = {}, {}, {}, {}
    ahead[0] = send(halves[0], to_even)
    z[0] = send(own[0], down)
    z[1] = send(own[1], down)
    own_two, z[0] = after(own[2], z[0])
    z[2] = send(own_two, down)
    up[0] = send(z[0], to_odd)
    own_three, z[1] = after(own[3], z[1])
    z[3] = send(own_three, down)
    up[1] = send(z[1], to_odd)
    own_high, ahead[0], z[1], *masks = after(halves[1], ahead[0], z[1], *masks)
    ahead[1] = send(own_high, to_even)
    outs = near(None, 0)
    up[2] = send(z[2], to_odd)
    up[1], *outs = after(up[1], *outs)
    z[4] = send(pick(z[0], up[1]), down)
    outs = near(outs, 1)
    up[3] = send(z[3], to_odd)
    z_one, ahead[1] = after(z[1], ahead[1])
    back[1] = send(z_one, to_even)
    up[2], *outs = after(up[2], *outs)
    z[5] = send(pick(ahead[0][:per_chunk], up[2]), down)
    up[4] = send(z[4], to_odd)
    z_two, back[1] = after(z[2], back[1])
    back[2] = send(z_two, to_even)
    outs = near(outs, 2)
    up[3], *outs = after(up[3], *outs)
    z[6] = send(up[3], down_odd)
    outs = near(outs, 3)
    z_three, back[2], *outs = after(z[3], back[2], *outs)
    back[3] = send(z_three, to_even)
    outs = far(outs, 1, 1)
    outs = far(outs, 2, 1)
    outs = far(outs, 0, 1)
    outs = far(outs, 3, 1)
    return tuple(outs)


def solution(mesh):
    placed = (P("tm", ("grp", "fiber"), None), P(("grp", "fiber")), P(("grp", "fiber")))
    return jax.shard_map(
        body,
        mesh=mesh,
        in_specs=placed,
        out_specs=(P("tm", ("grp", "fiber"), None), P("tm", ("grp", "fiber"), None)),
        check_vma=False,
    )
```

```python
import functools
import math

import jax
import jax.numpy as jnp
import ml_dtypes
import numpy as np
from jax import lax
from jax.experimental import pallas as pl
from jax.experimental.pallas import tpu as pltpu
from jax.sharding import PartitionSpec as P

FREQS = 32
FIRST_BIN = 8
LANES = 128
HOPS = 3
ROWS = 64
VMEM = 16 << 20


def make_table(length, bins, first_bin):
    steps_index = np.arange(length, dtype=np.int32)
    bin_index = np.arange(bins, dtype=np.int32) + first_bin
    products = bin_index[:, None] * steps_index[None, :] % length
    phases = (2.0 * math.pi * products / length).astype(np.float32)
    taper = 0.5 - 0.5 * np.cos((2.0 * math.pi * steps_index / length).astype(np.float32))
    taper = taper.astype(np.float32)
    cosines = taper[None, :] * np.cos(phases)
    sines = -taper[None, :] * np.sin(phases)
    return np.concatenate([cosines, sines], axis=0).astype(ml_dtypes.bfloat16)


def spectra_kernel(place_ref, samples_ref, table_ref, mine_ref, other_ref, raw_ref):
    windows, block, _ = samples_ref.shape
    pairs = mine_ref.shape[0]
    here = place_ref[0]
    tiles = raw_ref.shape[0]
    channel = lax.broadcasted_iota(jnp.int32, (1, block), 1)
    active = (channel < place_ref[1]).astype(jnp.float32)
    for w in range(windows):
        raw = lax.dot_general(
            table_ref[...], samples_ref[w], (((1,), (1,)), ((), ())),
            preferred_element_type=jnp.float32,
        )
        level = jnp.sum(raw * raw, axis=0, keepdims=True) * (1.0 / FREQS)
        white = raw * (lax.rsqrt(level + 1e-06) * active)
        for tile in range(tiles):
            start = tile * LANES
            width = min(LANES, block - start)
            raw_ref[tile, w * 2 * FREQS : (w + 1) * 2 * FREQS, :width] = white[:, start : start + width]
    for out_ref, first in ((mine_ref, here * 2 * pairs), (other_ref, (1 - here) * 2 * pairs)):
        for pair in range(pairs):
            for tile in range(tiles):
                start = tile * LANES
                width = min(LANES, block - start)
                rows = [
                    raw_ref[tile, pl.ds(first + 2 * pair + part, windows, stride=2 * FREQS), :]
                    for part in (0, FREQS, 1, FREQS + 1)
                ]
                turned = jnp.concatenate(rows, axis=0).T
                out_ref[pair, start : start + width, :] = turned[:width].astype(jnp.bfloat16)


def merge_kernel(mine_ref, theirs_ref, *out_refs, total_windows):
    block, lanes = mine_ref.shape[1:]
    half = lanes // 2
    lane = lax.broadcasted_iota(jnp.int32, (block, lanes), 1)
    per_chunk = out_refs[0].shape[0]
    for pair in range(mine_ref.shape[0]):
        mine = mine_ref[pair].astype(jnp.float32)
        theirs = theirs_ref[pair].astype(jnp.float32)
        both = (
            jnp.where(lane < half, mine, pltpu.roll(theirs, half, 1)),
            jnp.where(lane < half, pltpu.roll(mine, half, 1), theirs),
        )
        for step, values in enumerate(both):
            power = jnp.sum(values * values, axis=1, keepdims=True)
            root = lax.rsqrt(power * (1.0 / total_windows) + 1e-06)
            bin_at = 2 * pair + step
            out_refs[bin_at // per_chunk][bin_at % per_chunk] = (values * root).astype(jnp.bfloat16)


def band_kernel(*refs, own_first, places, hops, first_tile, total_windows):
    step = pl.program_id(0)
    own_ref, mask_ref = refs[:2]
    real_ref, imag_ref, right_ref, left_ref = refs[-4:]
    _, block, depth = own_ref.shape
    reach = min(HOPS * block - first_tile * LANES, real_ref.shape[2])
    origin = hops[0] * block
    filled = len(hops) * block
    parity = lax.rem(lax.axis_index("fiber"), 2)
    own = own_ref[own_first + step]
    if hops[0] == 0:
        right_ref[:block] = own
    if right_ref.shape[0] > filled:
        right_ref[filled:] = jnp.zeros((right_ref.shape[0] - filled, depth), jnp.bfloat16)

    def gather(odd):
        for hop, place in zip([hop for hop in hops if hop], places):
            operand, first_bin = place[odd]
            start = hop * block - origin
            right_ref[start : start + block] = refs[operand][first_bin + step]

    pl.when(parity == 0)(lambda: gather(0))
    pl.when(parity == 1)(lambda: gather(1))

    wide = own.astype(jnp.float32) * (1.0 / math.sqrt(total_windows))
    part = depth // 4
    lane = lax.broadcasted_iota(jnp.int32, (block, depth), 1)
    turned = jnp.where(
        (lane // part) % 2 == 0, pltpu.roll(wide, depth - part, 1), -pltpu.roll(wide, part, 1)
    )
    for group in range(block // ROWS):
        rows = slice(group * ROWS, (group + 1) * ROWS)
        left_ref[2 * group * ROWS : (2 * group + 1) * ROWS] = wide[rows].astype(jnp.bfloat16)
        left_ref[(2 * group + 1) * ROWS : (2 * group + 2) * ROWS] = turned[rows].astype(jnp.bfloat16)
    lane_of = lax.broadcasted_iota(jnp.int32, (ROWS, LANES), 1)
    row_of = lax.broadcasted_iota(jnp.int32, (ROWS, LANES), 0)
    out_tiles = -(-reach // LANES)
    mask_from = 2 if first_tile == 0 else 0
    for group in range(block // ROWS):
        first = group * ROWS
        begin = first + 1 + first_tile * LANES - origin
        base = begin // LANES
        shift = begin - base * LANES + row_of
        tiles = (begin + ROWS - 2 + reach) // LANES - base + 1
        products = lax.dot_general(
            left_ref[2 * first : 2 * first + 2 * ROWS],
            right_ref[base * LANES : (base + tiles) * LANES],
            (((1,), (1,)), ((), ())),
            preferred_element_type=jnp.float32,
        )
        keep = lane_of >= shift
        source = (lane_of + shift) % LANES
        for out_at, out_ref in enumerate((real_ref, imag_ref)):
            rows = products[out_at * ROWS : (out_at + 1) * ROWS]
            for tile in range(out_tiles):
                start = tile * LANES
                width = min(LANES, reach - start)
                values = rows[:, start : start + LANES]
                if tile + 1 < tiles:
                    values = jnp.where(keep, values, rows[:, start + LANES : start + 2 * LANES])
                moved = jnp.take_along_axis(values, source, axis=1, mode="promise_in_bounds")
                moved = moved.astype(jnp.bfloat16)
                if tile >= mask_from:
                    column = (tile - mask_from) * LANES
                    moved = moved * mask_ref[first : first + ROWS, column : column + LANES]
                out_ref[0, first : first + ROWS, start : start + width] = moved[:, :width]


def band(first_bin, bins, far, own, places, mask, so_far, bins_here, total_windows):
    _, block, depth = own[0].shape
    out = jax.ShapeDtypeStruct((bins_here, block, HOPS * block), jnp.bfloat16)
    near_width = 2 * block
    hops = (2, 3) if far else (0, 1, 2)
    out_spec = pl.BlockSpec((1, block, near_width), lambda i: (first_bin + i, 0, 1 if far else 0))
    operands = [own[0], mask]

    def index_of(array):
        for at, operand in enumerate(operands):
            if operand is array:
                return at
        operands.append(array)
        return len(operands) - 1

    places = [tuple((index_of(array), offset) for array, offset in place) for place in places]
    in_specs = [pl.BlockSpec(memory_space=pltpu.VMEM)] * len(operands)
    aliases = {}
    if so_far is not None:
        aliases = {len(operands): 0, len(operands) + 1: 1}
        operands += list(so_far)
        in_specs += [pl.BlockSpec(memory_space=pl.ANY)] * 2
    wide = block if far else near_width
    return pl.pallas_call(
        functools.partial(
            band_kernel,
            own_first=own[1],
            places=places,
            hops=hops,
            first_tile=near_width // LANES if far else 0,
            total_windows=total_windows,
        ),
        grid=(bins,),
        in_specs=in_specs,
        out_specs=[out_spec, out_spec],
        scratch_shapes=[
            pltpu.VMEM((-(-len(hops) * block // LANES) * LANES, depth), jnp.bfloat16),
            pltpu.VMEM((2 * block, depth), jnp.bfloat16),
        ],
        out_shape=[out, out],
        input_output_aliases=aliases,
        cost_estimate=pl.CostEstimate(
            flops=bins * 4 * block * wide * depth,
            bytes_accessed=bins * 4 * block * wide,
            transcendentals=0,
        ),
        compiler_params=pltpu.CompilerParams(vmem_limit_bytes=VMEM),
    )(*operands)


def body(samples, counts, reach_limit):
    windows_here, block, length = samples.shape
    tm_size = lax.axis_size("tm")
    fiber_size = lax.axis_size("fiber")
    total_windows = windows_here * tm_size
    bins_here = FREQS // tm_size
    lanes = 4 * windows_here
    here = lax.axis_index("tm").astype(jnp.int32)
    is_even = lax.axis_index("fiber") % 2 == 0

    pair_shape = jax.ShapeDtypeStruct((bins_here // 2, block, lanes), jnp.bfloat16)
    mine, other = pl.pallas_call(
        spectra_kernel,
        in_specs=[
            pl.BlockSpec(memory_space=pltpu.SMEM),
            pl.BlockSpec(memory_space=pltpu.VMEM),
            pl.BlockSpec(memory_space=pltpu.VMEM),
        ],
        out_specs=[pl.BlockSpec(memory_space=pltpu.VMEM)] * 2,
        out_shape=[pair_shape, pair_shape],
        scratch_shapes=[
            pltpu.VMEM((-(-block // LANES), windows_here * 2 * FREQS, LANES), jnp.float32)
        ],
        compiler_params=pltpu.CompilerParams(vmem_limit_bytes=VMEM),
    )(
        jnp.stack([here, counts[0]]),
        samples,
        jnp.asarray(make_table(length, FREQS, FIRST_BIN)),
    )
    theirs = lax.ppermute(other, "tm", [(0, 1), (1, 0)])
    half = bins_here // 2
    quarter = half // 2
    half_shape = jax.ShapeDtypeStruct((half, block, lanes), jnp.bfloat16)
    own = pl.pallas_call(
        functools.partial(merge_kernel, total_windows=total_windows),
        in_specs=[pl.BlockSpec(memory_space=pltpu.VMEM)] * 2,
        out_specs=[pl.BlockSpec(memory_space=pltpu.VMEM)] * 2,
        out_shape=[half_shape] * 2,
        compiler_params=pltpu.CompilerParams(vmem_limit_bytes=32 << 20),
    )(mine, theirs)

    down = [(i, i - 2) for i in range(2, fiber_size)]
    down_odd = [(i, i - 2) for i in range(3, fiber_size, 2)]
    to_even = [(i, i - 1) for i in range(1, fiber_size, 2)]
    to_odd = [(i - 1, i) for i in range(1, fiber_size, 2)]

    def pick(for_even, for_odd):
        even_one, for_even, for_odd = lax.optimization_barrier((is_even, for_even, for_odd))
        return lax.optimization_barrier(jnp.where(even_one, for_even, for_odd))

    def send(payload, route):
        return lax.ppermute(payload, "fiber", route)

    def after(payload, *others):
        return lax.optimization_barrier((payload, *others))

    near_reach = 2 * block
    offsets = jnp.arange(1, near_reach + HOPS * LANES + 1, dtype=jnp.int32)
    mask = (offsets[None, :] <= reach_limit[:, None]).astype(jnp.bfloat16)
    masks = (mask[:, 2 * LANES : near_reach], mask[:, near_reach:])

    def near(outs, at, one, two):
        return band(
            at * half, half, 0, (own[at], 0), (one, two), masks[0], outs, bins_here, total_windows
        )

    def far(outs, at, first, bins, two, three):
        return band(
            at * half + first, bins, 1, (own[at], first), (two, three), masks[1], outs, bins_here,
            total_windows,
        )

    ahead_low = send(own[0], to_even)
    z_low = send(own[0], down)
    own_high, ahead_low, *masks = after(own[1], ahead_low, *masks)
    z_high = send(own_high, down)
    y_low = send(z_low, to_even + to_odd)
    up_high = send(z_high, to_odd)
    own_high, y_low = after(own[1], y_low)
    ahead_high = send(own_high, to_even)
    z_next = send(y_low, down_odd)
    outs = near(None, 0, ((ahead_low, 0), (y_low, 0)), ((z_low, 0), (z_low, 0)))
    up_high, *outs = after(up_high, *outs)
    last = [
        send(pick(ahead_high[at : at + quarter], up_high[at : at + quarter]), down)
        for at in (0, quarter)
    ]
    outs = near(outs, 1, ((ahead_high, 0), (up_high, 0)), ((z_high, 0), (z_high, 0)))
    outs = far(outs, 0, 0, half, ((z_low, 0), (z_low, 0)), ((y_low, 0), (z_next, 0)))
    for part, at in enumerate((0, quarter)):
        outs = far(
            outs, 1, at, quarter, ((z_high, at), (z_high, at)), ((last[part], 0), (last[part], 0))
        )
    return tuple(outs)


def solution(mesh):
    placed = (P("tm", ("grp", "fiber"), None), P(("grp", "fiber")), P(("grp", "fiber")))
    return jax.shard_map(
        body,
        mesh=mesh,
        in_specs=placed,
        out_specs=(P("tm", ("grp", "fiber"), None), P("tm", ("grp", "fiber"), None)),
        check_vma=False,
    )
```

```python
import functools
import math

import jax
import jax.numpy as jnp
import ml_dtypes
import numpy as np
from jax import lax
from jax.experimental import pallas as pl
from jax.experimental.pallas import tpu as pltpu
from jax.sharding import PartitionSpec as P

FREQS = 32
FIRST_BIN = 8
LANES = 128
HOPS = 3
ROWS = 64
AT_ONCE = 1
VMEM = 16 << 20


def make_table(length, bins, first_bin):
    steps_index = np.arange(length, dtype=np.int32)
    bin_index = np.arange(bins, dtype=np.int32) + first_bin
    products = bin_index[:, None] * steps_index[None, :] % length
    phases = (2.0 * math.pi * products / length).astype(np.float32)
    taper = 0.5 - 0.5 * np.cos((2.0 * math.pi * steps_index / length).astype(np.float32))
    taper = taper.astype(np.float32)
    cosines = taper[None, :] * np.cos(phases)
    sines = -taper[None, :] * np.sin(phases)
    return np.concatenate([cosines, sines], axis=0).astype(ml_dtypes.bfloat16)


def spectra_kernel(place_ref, samples_ref, table_ref, mine_ref, other_ref, raw_ref):
    windows, block, _ = samples_ref.shape
    pairs = mine_ref.shape[0]
    here = place_ref[0]
    tiles = raw_ref.shape[0]
    channel = lax.broadcasted_iota(jnp.int32, (1, block), 1)
    active = (channel < place_ref[1]).astype(jnp.float32)
    for w in range(windows):
        raw = lax.dot_general(
            table_ref[...], samples_ref[w], (((1,), (1,)), ((), ())),
            preferred_element_type=jnp.float32,
        )
        level = jnp.sum(raw * raw, axis=0, keepdims=True) * (1.0 / FREQS)
        white = raw * (lax.rsqrt(level + 1e-06) * active)
        for tile in range(tiles):
            start = tile * LANES
            width = min(LANES, block - start)
            raw_ref[tile, w * 2 * FREQS : (w + 1) * 2 * FREQS, :width] = white[:, start : start + width]
    for out_ref, first in ((mine_ref, here * 2 * pairs), (other_ref, (1 - here) * 2 * pairs)):
        for pair in range(pairs):
            for tile in range(tiles):
                start = tile * LANES
                width = min(LANES, block - start)
                rows = [
                    raw_ref[tile, pl.ds(first + 2 * pair + part, windows, stride=2 * FREQS), :]
                    for part in (0, FREQS, 1, FREQS + 1)
                ]
                turned = jnp.concatenate(rows, axis=0).T
                out_ref[pair, start : start + width, :] = turned[:width].astype(jnp.bfloat16)


def merge_kernel(mine_ref, theirs_ref, *out_refs, total_windows):
    block, lanes = mine_ref.shape[1:]
    half = lanes // 2
    lane = lax.broadcasted_iota(jnp.int32, (block, lanes), 1)
    per_chunk = out_refs[0].shape[0]
    for pair in range(mine_ref.shape[0]):
        mine = mine_ref[pair].astype(jnp.float32)
        theirs = theirs_ref[pair].astype(jnp.float32)
        both = (
            jnp.where(lane < half, mine, pltpu.roll(theirs, half, 1)),
            jnp.where(lane < half, pltpu.roll(mine, half, 1), theirs),
        )
        for step, values in enumerate(both):
            power = jnp.sum(values * values, axis=1, keepdims=True)
            root = lax.rsqrt(power * (1.0 / total_windows) + 1e-06)
            bin_at = 2 * pair + step
            out_refs[bin_at // per_chunk][bin_at % per_chunk] = (values * root).astype(jnp.bfloat16)


def band_kernel(*refs, own_first, places, hops, first_tile, total_windows):
    own_ref = refs[0]
    real_ref, _, right_ref, _ = refs[-4:]
    at_once, block, _ = real_ref.shape
    depth = right_ref.shape[2]
    start_bin = pl.program_id(0) * at_once
    origin = hops[0] * block
    filled = len(hops) * block
    parity = lax.rem(lax.axis_index("fiber"), 2)

    def gather(odd):
        for inner in range(at_once):
            for hop, place in zip([hop for hop in hops if hop], places):
                operand, first_bin = place[odd]
                start = hop * block - origin
                right_ref[inner, start : start + block] = refs[operand][
                    first_bin + start_bin + inner
                ]

    pl.when(parity == 0)(lambda: gather(0))
    pl.when(parity == 1)(lambda: gather(1))
    for inner in range(at_once):
        own = own_ref[own_first + start_bin + inner]
        if hops[0] == 0:
            right_ref[inner, :block] = own
        if right_ref.shape[1] > filled:
            padding = (right_ref.shape[1] - filled, depth)
            right_ref[inner, filled:] = jnp.zeros(padding, jnp.bfloat16)
        one_bin(refs, own, inner, hops, first_tile, total_windows)


def one_bin(refs, own, inner, hops, first_tile, total_windows):
    mask_ref = refs[1]
    real_ref, imag_ref, right_all, left_all = refs[-4:]
    right_ref, left_ref = right_all.at[inner], left_all.at[inner]
    block, depth = own.shape
    reach = min(HOPS * block - first_tile * LANES, real_ref.shape[2])
    origin = hops[0] * block
    wide = own.astype(jnp.float32) * (1.0 / math.sqrt(total_windows))
    part = depth // 4
    lane = lax.broadcasted_iota(jnp.int32, (block, depth), 1)
    turned = jnp.where(
        (lane // part) % 2 == 0, pltpu.roll(wide, depth - part, 1), -pltpu.roll(wide, part, 1)
    )
    for first in range(0, block, ROWS):
        count = min(ROWS, block - first)
        rows = slice(first, first + count)
        left_ref[2 * first : 2 * first + count] = wide[rows].astype(jnp.bfloat16)
        left_ref[2 * first + count : 2 * (first + count)] = turned[rows].astype(jnp.bfloat16)
    out_tiles = -(-reach // LANES)
    mask_from = 2 if first_tile == 0 else 0
    for first in range(0, block, ROWS):
        count = min(ROWS, block - first)
        lane_of = lax.broadcasted_iota(jnp.int32, (count, LANES), 1)
        row_of = lax.broadcasted_iota(jnp.int32, (count, LANES), 0)
        begin = first + 1 + first_tile * LANES - origin
        base = begin // LANES
        shift = begin - base * LANES + row_of
        tiles = (begin + count - 2 + reach) // LANES - base + 1
        products = lax.dot_general(
            left_ref[2 * first : 2 * (first + count)],
            right_ref[base * LANES : (base + tiles) * LANES],
            (((1,), (1,)), ((), ())),
            preferred_element_type=jnp.float32,
        )
        keep = lane_of >= shift
        source = (lane_of + shift) % LANES
        for out_at, out_ref in enumerate((real_ref, imag_ref)):
            rows = products[out_at * count : (out_at + 1) * count]
            for tile in range(out_tiles):
                start = tile * LANES
                width = min(LANES, reach - start)
                values = rows[:, start : start + LANES]
                if tile + 1 < tiles:
                    values = jnp.where(keep, values, rows[:, start + LANES : start + 2 * LANES])
                moved = jnp.take_along_axis(values, source, axis=1, mode="promise_in_bounds")
                moved = moved.astype(jnp.bfloat16)
                if tile >= mask_from:
                    column = (tile - mask_from) * LANES
                    moved = moved * mask_ref[first : first + count, column : column + LANES]
                out_ref[inner, first : first + count, start : start + width] = moved[:, :width]


def band(first_bin, bins, far, own, places, mask, so_far, bins_here, total_windows):
    _, block, depth = own[0].shape
    out = jax.ShapeDtypeStruct((bins_here, block, HOPS * block), jnp.bfloat16)
    near_width = 2 * block
    hops = (2, 3) if far else (0, 1, 2)
    out_spec = pl.BlockSpec(
        (AT_ONCE, block, near_width), lambda i: (first_bin // AT_ONCE + i, 0, 1 if far else 0)
    )
    operands = [own[0], mask]

    def index_of(array):
        for at, operand in enumerate(operands):
            if operand is array:
                return at
        operands.append(array)
        return len(operands) - 1

    places = [tuple((index_of(array), offset) for array, offset in place) for place in places]
    in_specs = [pl.BlockSpec(memory_space=pltpu.VMEM)] * len(operands)
    aliases = {}
    if so_far is not None:
        aliases = {len(operands): 0, len(operands) + 1: 1}
        operands += list(so_far)
        in_specs += [pl.BlockSpec(memory_space=pl.ANY)] * 2
    wide = block if far else near_width
    return pl.pallas_call(
        functools.partial(
            band_kernel,
            own_first=own[1],
            places=places,
            hops=hops,
            first_tile=near_width // LANES if far else 0,
            total_windows=total_windows,
        ),
        grid=(bins // AT_ONCE,),
        in_specs=in_specs,
        out_specs=[out_spec, out_spec],
        scratch_shapes=[
            pltpu.VMEM((AT_ONCE, -(-len(hops) * block // LANES) * LANES, depth), jnp.bfloat16),
            pltpu.VMEM((AT_ONCE, 2 * block, depth), jnp.bfloat16),
        ],
        out_shape=[out, out],
        input_output_aliases=aliases,
        cost_estimate=pl.CostEstimate(
            flops=bins * 4 * block * wide * depth,
            bytes_accessed=bins * 4 * block * wide,
            transcendentals=0,
        ),
        compiler_params=pltpu.CompilerParams(vmem_limit_bytes=VMEM),
    )(*operands)


def body(samples, counts, reach_limit):
    windows_here, block, length = samples.shape
    tm_size = lax.axis_size("tm")
    fiber_size = lax.axis_size("fiber")
    total_windows = windows_here * tm_size
    bins_here = FREQS // tm_size
    lanes = 4 * windows_here
    here = lax.axis_index("tm").astype(jnp.int32)
    is_even = lax.axis_index("fiber") % 2 == 0

    pair_shape = jax.ShapeDtypeStruct((bins_here // 2, block, lanes), jnp.bfloat16)
    mine, other = pl.pallas_call(
        spectra_kernel,
        in_specs=[
            pl.BlockSpec(memory_space=pltpu.SMEM),
            pl.BlockSpec(memory_space=pltpu.VMEM),
            pl.BlockSpec(memory_space=pltpu.VMEM),
        ],
        out_specs=[pl.BlockSpec(memory_space=pltpu.VMEM)] * 2,
        out_shape=[pair_shape, pair_shape],
        scratch_shapes=[
            pltpu.VMEM((-(-block // LANES), windows_here * 2 * FREQS, LANES), jnp.float32)
        ],
        compiler_params=pltpu.CompilerParams(vmem_limit_bytes=VMEM),
    )(
        jnp.stack([here, counts[0]]),
        samples,
        jnp.asarray(make_table(length, FREQS, FIRST_BIN)),
    )
    theirs = lax.ppermute(other, "tm", [(0, 1), (1, 0)])
    half = bins_here // 2
    quarter = half // 2
    half_shape = jax.ShapeDtypeStruct((half, block, lanes), jnp.bfloat16)
    own = pl.pallas_call(
        functools.partial(merge_kernel, total_windows=total_windows),
        in_specs=[pl.BlockSpec(memory_space=pltpu.VMEM)] * 2,
        out_specs=[pl.BlockSpec(memory_space=pltpu.VMEM)] * 2,
        out_shape=[half_shape] * 2,
        compiler_params=pltpu.CompilerParams(vmem_limit_bytes=32 << 20),
    )(mine, theirs)

    down = [(i, i - 2) for i in range(2, fiber_size)]
    down_odd = [(i, i - 2) for i in range(3, fiber_size, 2)]
    to_even = [(i, i - 1) for i in range(1, fiber_size, 2)]
    to_odd = [(i - 1, i) for i in range(1, fiber_size, 2)]

    def pick(for_even, for_odd):
        even_one, for_even, for_odd = lax.optimization_barrier((is_even, for_even, for_odd))
        return lax.optimization_barrier(jnp.where(even_one, for_even, for_odd))

    def send(payload, route):
        return lax.ppermute(payload, "fiber", route)

    def after(payload, *others):
        return lax.optimization_barrier((payload, *others))

    near_reach = 2 * block
    offsets = jnp.arange(1, near_reach + HOPS * LANES + 1, dtype=jnp.int32)
    mask = (offsets[None, :] <= reach_limit[:, None]).astype(jnp.bfloat16)
    masks = (mask[:, 2 * LANES : near_reach], mask[:, near_reach:])

    def near(outs, chunk, one, two):
        mine = (own[chunk // 2], chunk % 2 * quarter)
        return band(
            chunk * quarter, quarter, 0, mine, (one, two), masks[0], outs, bins_here, total_windows
        )

    def far(outs, chunk, two, three):
        mine = (own[chunk // 2], chunk % 2 * quarter)
        return band(
            chunk * quarter, quarter, 1, mine, (two, three), masks[1], outs, bins_here,
            total_windows,
        )

    def both(array, first=0):
        return ((array, first), (array, first))

    ahead_low = send(own[0], to_even)
    z_zero = send(own[0][:quarter], down)
    z_payload, z_zero = after(own[0][quarter:], z_zero)
    z_one = send(z_payload, down)
    y_zero = send(z_zero, to_even + to_odd)
    own_high, z_one, ahead_low, *masks = after(own[1], z_one, ahead_low, *masks)
    z_high = send(own_high, down)
    z_one, y_zero = after(z_one, y_zero)
    y_one = send(z_one, to_even + to_odd)
    outs = near(None, 0, ((ahead_low, 0), (y_zero, 0)), both(z_zero))
    own_high, y_one = after(own[1], y_one)
    ahead_high = send(own_high, to_even)
    outs = near(outs, 1, ((ahead_low, quarter), (y_one, 0)), both(z_one))
    y_one, z_high, *outs = after(y_one, z_high, *outs)
    up_two = send(z_high[:quarter], to_odd)
    z_next = send(pick(z_zero, y_one), down)
    z_three, up_two = after(z_high[quarter:], up_two)
    up_three = send(z_three, to_odd)
    last_two = send(pick(ahead_high[:quarter], up_two), down)
    up_next = send(z_next, to_odd)
    outs = near(outs, 2, ((ahead_high, 0), (up_two, 0)), both(z_high))
    up_three, *outs = after(up_three, *outs)
    last_three = send(pick(ahead_high[quarter:], up_three), down)
    outs = far(outs, 1, both(z_one), ((y_one, 0), (z_next, 0)))
    outs = near(outs, 3, ((ahead_high, quarter), (up_three, 0)), both(z_high, quarter))
    outs = far(outs, 0, both(z_zero), ((y_zero, 0), (up_next, 0)))
    outs = far(outs, 2, both(z_high), both(last_two))
    outs = far(outs, 3, both(z_high, quarter), both(last_three))
    return tuple(outs)


def solution(mesh):
    placed = (P("tm", ("grp", "fiber"), None), P(("grp", "fiber")), P(("grp", "fiber")))
    return jax.shard_map(
        body,
        mesh=mesh,
        in_specs=placed,
        out_specs=(P("tm", ("grp", "fiber"), None), P("tm", ("grp", "fiber"), None)),
        check_vma=False,
    )
```

```python
import functools
import math

import jax
import jax.numpy as jnp
import ml_dtypes
import numpy as np
from jax import lax
from jax.experimental import pallas as pl
from jax.experimental.pallas import tpu as pltpu
from jax.sharding import PartitionSpec as P

FREQS = 32
FIRST_BIN = 8
LANES = 128
HOPS = 3
ROWS = 64
AT_ONCE = 2
VMEM = 16 << 20


def make_table(length, bins, first_bin):
    steps_index = np.arange(length, dtype=np.int32)
    bin_index = np.arange(bins, dtype=np.int32) + first_bin
    products = bin_index[:, None] * steps_index[None, :] % length
    phases = (2.0 * math.pi * products / length).astype(np.float32)
    taper = 0.5 - 0.5 * np.cos((2.0 * math.pi * steps_index / length).astype(np.float32))
    taper = taper.astype(np.float32)
    cosines = taper[None, :] * np.cos(phases)
    sines = -taper[None, :] * np.sin(phases)
    return np.concatenate([cosines, sines], axis=0).astype(ml_dtypes.bfloat16)


def spectra_kernel(place_ref, samples_ref, table_ref, mine_ref, other_ref, raw_ref):
    windows, block, _ = samples_ref.shape
    pairs = mine_ref.shape[0]
    here = place_ref[0]
    tiles = raw_ref.shape[0]
    channel = lax.broadcasted_iota(jnp.int32, (1, block), 1)
    active = (channel < place_ref[1]).astype(jnp.float32)
    for w in range(windows):
        raw = lax.dot_general(
            table_ref[...], samples_ref[w], (((1,), (1,)), ((), ())),
            preferred_element_type=jnp.float32,
        )
        level = jnp.sum(raw * raw, axis=0, keepdims=True) * (1.0 / FREQS)
        white = raw * (lax.rsqrt(level + 1e-06) * active)
        for tile in range(tiles):
            start = tile * LANES
            width = min(LANES, block - start)
            raw_ref[tile, w * 2 * FREQS : (w + 1) * 2 * FREQS, :width] = white[:, start : start + width]
    for out_ref, first in ((mine_ref, here * 2 * pairs), (other_ref, (1 - here) * 2 * pairs)):
        for pair in range(pairs):
            for tile in range(tiles):
                start = tile * LANES
                width = min(LANES, block - start)
                rows = [
                    raw_ref[tile, pl.ds(first + 2 * pair + part, windows, stride=2 * FREQS), :]
                    for part in (0, FREQS, 1, FREQS + 1)
                ]
                turned = jnp.concatenate(rows, axis=0).T
                out_ref[pair, start : start + width, :] = turned[:width].astype(jnp.bfloat16)


def merge_kernel(mine_ref, theirs_ref, *out_refs, total_windows):
    block, lanes = mine_ref.shape[1:]
    half = lanes // 2
    lane = lax.broadcasted_iota(jnp.int32, (block, lanes), 1)
    per_chunk = out_refs[0].shape[0]
    for pair in range(mine_ref.shape[0]):
        mine = mine_ref[pair].astype(jnp.float32)
        theirs = theirs_ref[pair].astype(jnp.float32)
        both = (
            jnp.where(lane < half, mine, pltpu.roll(theirs, half, 1)),
            jnp.where(lane < half, pltpu.roll(mine, half, 1), theirs),
        )
        for step, values in enumerate(both):
            power = jnp.sum(values * values, axis=1, keepdims=True)
            root = lax.rsqrt(power * (1.0 / total_windows) + 1e-06)
            bin_at = 2 * pair + step
            out_refs[bin_at // per_chunk][bin_at % per_chunk] = (values * root).astype(jnp.bfloat16)


def band_kernel(*refs, own_first, places, hops, first_tile, total_windows):
    own_ref = refs[0]
    real_ref, _, right_ref, _ = refs[-4:]
    at_once, block, _ = real_ref.shape
    depth = right_ref.shape[2]
    start_bin = pl.program_id(0) * at_once
    origin = hops[0] * block
    filled = len(hops) * block
    parity = lax.rem(lax.axis_index("fiber"), 2)

    def gather(odd):
        for inner in range(at_once):
            for hop, place in zip([hop for hop in hops if hop], places):
                operand, first_bin = place[odd]
                start = hop * block - origin
                right_ref[inner, start : start + block] = refs[operand][
                    first_bin + start_bin + inner
                ]

    pl.when(parity == 0)(lambda: gather(0))
    pl.when(parity == 1)(lambda: gather(1))
    for inner in range(at_once):
        own = own_ref[own_first + start_bin + inner]
        if hops[0] == 0:
            right_ref[inner, :block] = own
        if right_ref.shape[1] > filled:
            padding = (right_ref.shape[1] - filled, depth)
            right_ref[inner, filled:] = jnp.zeros(padding, jnp.bfloat16)
        one_bin(refs, own, inner, hops, first_tile, total_windows)


def one_bin(refs, own, inner, hops, first_tile, total_windows):
    mask_ref = refs[1]
    real_ref, imag_ref, right_all, left_all = refs[-4:]
    right_ref, left_ref = right_all.at[inner], left_all.at[inner]
    block, depth = own.shape
    reach = min(HOPS * block - first_tile * LANES, real_ref.shape[2])
    origin = hops[0] * block
    wide = own.astype(jnp.float32) * (1.0 / math.sqrt(total_windows))
    part = depth // 4
    lane = lax.broadcasted_iota(jnp.int32, (block, depth), 1)
    turned = jnp.where(
        (lane // part) % 2 == 0, pltpu.roll(wide, depth - part, 1), -pltpu.roll(wide, part, 1)
    )
    for first in range(0, block, ROWS):
        count = min(ROWS, block - first)
        rows = slice(first, first + count)
        left_ref[2 * first : 2 * first + count] = wide[rows].astype(jnp.bfloat16)
        left_ref[2 * first + count : 2 * (first + count)] = turned[rows].astype(jnp.bfloat16)
    out_tiles = -(-reach // LANES)
    mask_from = 2 if first_tile == 0 else 0
    for first in range(0, block, ROWS):
        count = min(ROWS, block - first)
        lane_of = lax.broadcasted_iota(jnp.int32, (count, LANES), 1)
        row_of = lax.broadcasted_iota(jnp.int32, (count, LANES), 0)
        begin = first + 1 + first_tile * LANES - origin
        base = begin // LANES
        shift = begin - base * LANES + row_of
        tiles = (begin + count - 2 + reach) // LANES - base + 1
        products = lax.dot_general(
            left_ref[2 * first : 2 * (first + count)],
            right_ref[base * LANES : (base + tiles) * LANES],
            (((1,), (1,)), ((), ())),
            preferred_element_type=jnp.float32,
        )
        keep = lane_of >= shift
        source = (lane_of + shift) % LANES
        for out_at, out_ref in enumerate((real_ref, imag_ref)):
            rows = products[out_at * count : (out_at + 1) * count]
            for tile in range(out_tiles):
                start = tile * LANES
                width = min(LANES, reach - start)
                values = rows[:, start : start + LANES]
                if tile + 1 < tiles:
                    values = jnp.where(keep, values, rows[:, start + LANES : start + 2 * LANES])
                moved = jnp.take_along_axis(values, source, axis=1, mode="promise_in_bounds")
                moved = moved.astype(jnp.bfloat16)
                if tile >= mask_from:
                    column = (tile - mask_from) * LANES
                    moved = moved * mask_ref[first : first + count, column : column + LANES]
                out_ref[inner, first : first + count, start : start + width] = moved[:, :width]


def band(first_bin, bins, far, own, places, mask, so_far, bins_here, total_windows):
    _, block, depth = own[0].shape
    out = jax.ShapeDtypeStruct((bins_here, block, HOPS * block), jnp.bfloat16)
    near_width = 2 * block
    hops = (2, 3) if far else (0, 1, 2)
    out_spec = pl.BlockSpec(
        (AT_ONCE, block, near_width), lambda i: (first_bin // AT_ONCE + i, 0, 1 if far else 0)
    )
    operands = [own[0], mask]

    def index_of(array):
        for at, operand in enumerate(operands):
            if operand is array:
                return at
        operands.append(array)
        return len(operands) - 1

    places = [tuple((index_of(array), offset) for array, offset in place) for place in places]
    in_specs = [pl.BlockSpec(memory_space=pltpu.VMEM)] * len(operands)
    aliases = {}
    if so_far is not None:
        aliases = {len(operands): 0, len(operands) + 1: 1}
        operands += list(so_far)
        in_specs += [pl.BlockSpec(memory_space=pl.ANY)] * 2
    wide = block if far else near_width
    return pl.pallas_call(
        functools.partial(
            band_kernel,
            own_first=own[1],
            places=places,
            hops=hops,
            first_tile=near_width // LANES if far else 0,
            total_windows=total_windows,
        ),
        grid=(bins // AT_ONCE,),
        in_specs=in_specs,
        out_specs=[out_spec, out_spec],
        scratch_shapes=[
            pltpu.VMEM((AT_ONCE, -(-len(hops) * block // LANES) * LANES, depth), jnp.bfloat16),
            pltpu.VMEM((AT_ONCE, 2 * block, depth), jnp.bfloat16),
        ],
        out_shape=[out, out],
        input_output_aliases=aliases,
        cost_estimate=pl.CostEstimate(
            flops=bins * 4 * block * wide * depth,
            bytes_accessed=bins * 4 * block * wide,
            transcendentals=0,
        ),
        compiler_params=pltpu.CompilerParams(vmem_limit_bytes=VMEM),
    )(*operands)


def body(samples, counts, reach_limit):
    windows_here, block, length = samples.shape
    tm_size = lax.axis_size("tm")
    fiber_size = lax.axis_size("fiber")
    total_windows = windows_here * tm_size
    bins_here = FREQS // tm_size
    lanes = 4 * windows_here
    here = lax.axis_index("tm").astype(jnp.int32)
    is_even = lax.axis_index("fiber") % 2 == 0

    pair_shape = jax.ShapeDtypeStruct((bins_here // 2, block, lanes), jnp.bfloat16)
    mine, other = pl.pallas_call(
        spectra_kernel,
        in_specs=[
            pl.BlockSpec(memory_space=pltpu.SMEM),
            pl.BlockSpec(memory_space=pltpu.VMEM),
            pl.BlockSpec(memory_space=pltpu.VMEM),
        ],
        out_specs=[pl.BlockSpec(memory_space=pltpu.VMEM)] * 2,
        out_shape=[pair_shape, pair_shape],
        scratch_shapes=[
            pltpu.VMEM((-(-block // LANES), windows_here * 2 * FREQS, LANES), jnp.float32)
        ],
        compiler_params=pltpu.CompilerParams(vmem_limit_bytes=VMEM),
    )(
        jnp.stack([here, counts[0]]),
        samples,
        jnp.asarray(make_table(length, FREQS, FIRST_BIN)),
    )
    theirs = lax.ppermute(other, "tm", [(0, 1), (1, 0)])
    half = bins_here // 2
    quarter = half // 2
    half_shape = jax.ShapeDtypeStruct((half, block, lanes), jnp.bfloat16)
    own = pl.pallas_call(
        functools.partial(merge_kernel, total_windows=total_windows),
        in_specs=[pl.BlockSpec(memory_space=pltpu.VMEM)] * 2,
        out_specs=[pl.BlockSpec(memory_space=pltpu.VMEM)] * 2,
        out_shape=[half_shape] * 2,
        compiler_params=pltpu.CompilerParams(vmem_limit_bytes=32 << 20),
    )(mine, theirs)

    down = [(i, i - 2) for i in range(2, fiber_size)]
    down_odd = [(i, i - 2) for i in range(3, fiber_size, 2)]
    to_even = [(i, i - 1) for i in range(1, fiber_size, 2)]
    to_odd = [(i - 1, i) for i in range(1, fiber_size, 2)]

    def pick(for_even, for_odd):
        even_one, for_even, for_odd = lax.optimization_barrier((is_even, for_even, for_odd))
        return lax.optimization_barrier(jnp.where(even_one, for_even, for_odd))

    def send(payload, route):
        return lax.ppermute(payload, "fiber", route)

    def after(payload, *others):
        return lax.optimization_barrier((payload, *others))

    near_reach = 2 * block
    offsets = jnp.arange(1, near_reach + HOPS * LANES + 1, dtype=jnp.int32)
    mask = (offsets[None, :] <= reach_limit[:, None]).astype(jnp.bfloat16)
    masks = (mask[:, 2 * LANES : near_reach], mask[:, near_reach:])

    def near(outs, at, one, two):
        return band(
            at * half, half, 0, (own[at], 0), (one, two), masks[0], outs, bins_here, total_windows
        )

    def far(outs, at, first, bins, two, three):
        return band(
            at * half + first, bins, 1, (own[at], first), (two, three), masks[1], outs, bins_here,
            total_windows,
        )

    ahead_low = send(own[0], to_even)
    z_low = send(own[0], down)
    own_high, ahead_low, *masks = after(own[1], ahead_low, *masks)
    z_high = send(own_high, down)
    y_low = send(z_low, to_even + to_odd)
    up_high = send(z_high, to_odd)
    own_high, y_low = after(own[1], y_low)
    ahead_high = send(own_high, to_even)
    z_next = send(y_low, down_odd)
    outs = near(None, 0, ((ahead_low, 0), (y_low, 0)), ((z_low, 0), (z_low, 0)))
    up_high, *outs = after(up_high, *outs)
    last = [
        send(pick(ahead_high[at : at + quarter], up_high[at : at + quarter]), down)
        for at in (0, quarter)
    ]
    outs = near(outs, 1, ((ahead_high, 0), (up_high, 0)), ((z_high, 0), (z_high, 0)))
    outs = far(outs, 0, 0, half, ((z_low, 0), (z_low, 0)), ((y_low, 0), (z_next, 0)))
    for part, at in enumerate((0, quarter)):
        outs = far(
            outs, 1, at, quarter, ((z_high, at), (z_high, at)), ((last[part], 0), (last[part], 0))
        )
    return tuple(outs)


def solution(mesh):
    placed = (P("tm", ("grp", "fiber"), None), P(("grp", "fiber")), P(("grp", "fiber")))
    return jax.shard_map(
        body,
        mesh=mesh,
        in_specs=placed,
        out_specs=(P("tm", ("grp", "fiber"), None), P("tm", ("grp", "fiber"), None)),
        check_vma=False,
    )
```

```python
import functools
import math

import jax
import jax.numpy as jnp
import ml_dtypes
import numpy as np
from jax import lax
from jax.experimental import pallas as pl
from jax.experimental.pallas import tpu as pltpu
from jax.sharding import PartitionSpec as P

FREQS = 32
FIRST_BIN = 8
LANES = 128
HOPS = 3
ROWS = 64
AT_ONCE = 2
VMEM = 16 << 20


def make_table(length, bins, first_bin):
    steps_index = np.arange(length, dtype=np.int32)
    bin_index = np.arange(bins, dtype=np.int32) + first_bin
    products = bin_index[:, None] * steps_index[None, :] % length
    phases = (2.0 * math.pi * products / length).astype(np.float32)
    taper = 0.5 - 0.5 * np.cos((2.0 * math.pi * steps_index / length).astype(np.float32))
    taper = taper.astype(np.float32)
    cosines = taper[None, :] * np.cos(phases)
    sines = -taper[None, :] * np.sin(phases)
    return np.concatenate([cosines, sines], axis=0).astype(ml_dtypes.bfloat16)


def spectra_kernel(
    place_ref, samples_any, table_any, mine_ref, other_ref, raw_ref, samples_ref, table_ref, sems
):
    windows, block, _ = samples_ref.shape
    pairs = mine_ref.shape[0]
    here = place_ref[0]
    tiles = raw_ref.shape[0]
    groups = sems.shape[0] - 1
    at_once = windows // groups
    copies = [pltpu.make_async_copy(table_any, table_ref, sems.at[groups])]
    for group in range(groups):
        part = pl.ds(group * at_once, at_once)
        copies.append(
            pltpu.make_async_copy(samples_any.at[part], samples_ref.at[part], sems.at[group])
        )
    for copy in copies:
        copy.start()
    copies[0].wait()
    channel = lax.broadcasted_iota(jnp.int32, (1, block), 1)
    active = (channel < place_ref[1]).astype(jnp.float32)
    for w in range(windows):
        if w % at_once == 0:
            copies[1 + w // at_once].wait()
        raw = lax.dot_general(
            table_ref[...], samples_ref[w], (((1,), (1,)), ((), ())),
            preferred_element_type=jnp.float32,
        )
        level = jnp.sum(raw * raw, axis=0, keepdims=True) * (1.0 / FREQS)
        white = raw * (lax.rsqrt(level + 1e-06) * active)
        for tile in range(tiles):
            start = tile * LANES
            width = min(LANES, block - start)
            raw_ref[tile, w * 2 * FREQS : (w + 1) * 2 * FREQS, :width] = white[:, start : start + width]
    for out_ref, first in ((mine_ref, here * 2 * pairs), (other_ref, (1 - here) * 2 * pairs)):
        for pair in range(pairs):
            for tile in range(tiles):
                start = tile * LANES
                width = min(LANES, block - start)
                rows = [
                    raw_ref[tile, pl.ds(first + 2 * pair + part, windows, stride=2 * FREQS), :]
                    for part in (0, FREQS, 1, FREQS + 1)
                ]
                turned = jnp.concatenate(rows, axis=0).T
                out_ref[pair, start : start + width, :] = turned[:width].astype(jnp.bfloat16)


def merge_kernel(mine_ref, theirs_ref, *out_refs, total_windows):
    block, lanes = mine_ref.shape[1:]
    half = lanes // 2
    lane = lax.broadcasted_iota(jnp.int32, (block, lanes), 1)
    per_chunk = out_refs[0].shape[0]
    for pair in range(mine_ref.shape[0]):
        mine = mine_ref[pair].astype(jnp.float32)
        theirs = theirs_ref[pair].astype(jnp.float32)
        both = (
            jnp.where(lane < half, mine, pltpu.roll(theirs, half, 1)),
            jnp.where(lane < half, pltpu.roll(mine, half, 1), theirs),
        )
        for step, values in enumerate(both):
            power = jnp.sum(values * values, axis=1, keepdims=True)
            root = lax.rsqrt(power * (1.0 / total_windows) + 1e-06)
            bin_at = 2 * pair + step
            out_refs[bin_at // per_chunk][bin_at % per_chunk] = (values * root).astype(jnp.bfloat16)


def band_kernel(*refs, own_first, places, hops, first_tile, total_windows):
    own_ref = refs[0]
    real_ref, _, right_ref, _ = refs[-4:]
    at_once, block, _ = real_ref.shape
    depth = right_ref.shape[2]
    start_bin = pl.program_id(0) * at_once
    origin = hops[0] * block
    filled = len(hops) * block
    parity = lax.rem(lax.axis_index("fiber"), 2)

    def gather(odd):
        for inner in range(at_once):
            for hop, place in zip([hop for hop in hops if hop], places):
                operand, first_bin = place[odd]
                start = hop * block - origin
                right_ref[inner, start : start + block] = refs[operand][
                    first_bin + start_bin + inner
                ]

    pl.when(parity == 0)(lambda: gather(0))
    pl.when(parity == 1)(lambda: gather(1))
    for inner in range(at_once):
        own = own_ref[own_first + start_bin + inner]
        if hops[0] == 0:
            right_ref[inner, :block] = own
        if right_ref.shape[1] > filled:
            padding = (right_ref.shape[1] - filled, depth)
            right_ref[inner, filled:] = jnp.zeros(padding, jnp.bfloat16)
        one_bin(refs, own, inner, hops, first_tile, total_windows)


def one_bin(refs, own, inner, hops, first_tile, total_windows):
    mask_ref = refs[1]
    real_ref, imag_ref, right_all, left_all = refs[-4:]
    right_ref, left_ref = right_all.at[inner], left_all.at[inner]
    block, depth = own.shape
    reach = min(HOPS * block - first_tile * LANES, real_ref.shape[2])
    origin = hops[0] * block
    wide = own.astype(jnp.float32) * (1.0 / math.sqrt(total_windows))
    part = depth // 4
    lane = lax.broadcasted_iota(jnp.int32, (block, depth), 1)
    turned = jnp.where(
        (lane // part) % 2 == 0, pltpu.roll(wide, depth - part, 1), -pltpu.roll(wide, part, 1)
    )
    for first in range(0, block, ROWS):
        count = min(ROWS, block - first)
        rows = slice(first, first + count)
        left_ref[2 * first : 2 * first + count] = wide[rows].astype(jnp.bfloat16)
        left_ref[2 * first + count : 2 * (first + count)] = turned[rows].astype(jnp.bfloat16)
    out_tiles = -(-reach // LANES)
    mask_from = 2 if first_tile == 0 else 0
    for first in range(0, block, ROWS):
        count = min(ROWS, block - first)
        lane_of = lax.broadcasted_iota(jnp.int32, (count, LANES), 1)
        row_of = lax.broadcasted_iota(jnp.int32, (count, LANES), 0)
        begin = first + 1 + first_tile * LANES - origin
        base = begin // LANES
        shift = begin - base * LANES + row_of
        tiles = (begin + count - 2 + reach) // LANES - base + 1
        products = lax.dot_general(
            left_ref[2 * first : 2 * (first + count)],
            right_ref[base * LANES : (base + tiles) * LANES],
            (((1,), (1,)), ((), ())),
            preferred_element_type=jnp.float32,
        )
        keep = lane_of >= shift
        source = (lane_of + shift) % LANES
        for out_at, out_ref in enumerate((real_ref, imag_ref)):
            rows = products[out_at * count : (out_at + 1) * count]
            for tile in range(out_tiles):
                start = tile * LANES
                width = min(LANES, reach - start)
                values = rows[:, start : start + LANES]
                if tile + 1 < tiles:
                    values = jnp.where(keep, values, rows[:, start + LANES : start + 2 * LANES])
                moved = jnp.take_along_axis(values, source, axis=1, mode="promise_in_bounds")
                moved = moved.astype(jnp.bfloat16)
                if tile >= mask_from:
                    column = (tile - mask_from) * LANES
                    moved = moved * mask_ref[first : first + count, column : column + LANES]
                out_ref[inner, first : first + count, start : start + width] = moved[:, :width]


def band(first_bin, bins, far, own, places, mask, so_far, bins_here, total_windows):
    _, block, depth = own[0].shape
    out = jax.ShapeDtypeStruct((bins_here, block, HOPS * block), jnp.bfloat16)
    near_width = 2 * block
    hops = (2, 3) if far else (0, 1, 2)
    out_spec = pl.BlockSpec(
        (AT_ONCE, block, near_width), lambda i: (first_bin // AT_ONCE + i, 0, 1 if far else 0)
    )
    operands = [own[0], mask]

    def index_of(array):
        for at, operand in enumerate(operands):
            if operand is array:
                return at
        operands.append(array)
        return len(operands) - 1

    places = [tuple((index_of(array), offset) for array, offset in place) for place in places]
    in_specs = [pl.BlockSpec(memory_space=pltpu.VMEM)] * len(operands)
    aliases = {}
    if so_far is not None:
        aliases = {len(operands): 0, len(operands) + 1: 1}
        operands += list(so_far)
        in_specs += [pl.BlockSpec(memory_space=pl.ANY)] * 2
    wide = block if far else near_width
    return pl.pallas_call(
        functools.partial(
            band_kernel,
            own_first=own[1],
            places=places,
            hops=hops,
            first_tile=near_width // LANES if far else 0,
            total_windows=total_windows,
        ),
        grid=(bins // AT_ONCE,),
        in_specs=in_specs,
        out_specs=[out_spec, out_spec],
        scratch_shapes=[
            pltpu.VMEM((AT_ONCE, -(-len(hops) * block // LANES) * LANES, depth), jnp.bfloat16),
            pltpu.VMEM((AT_ONCE, 2 * block, depth), jnp.bfloat16),
        ],
        out_shape=[out, out],
        input_output_aliases=aliases,
        cost_estimate=pl.CostEstimate(
            flops=bins * 4 * block * wide * depth,
            bytes_accessed=bins * 4 * block * wide,
            transcendentals=0,
        ),
        compiler_params=pltpu.CompilerParams(vmem_limit_bytes=VMEM),
    )(*operands)


def body(samples, counts, reach_limit):
    windows_here, block, length = samples.shape
    tm_size = lax.axis_size("tm")
    fiber_size = lax.axis_size("fiber")
    total_windows = windows_here * tm_size
    bins_here = FREQS // tm_size
    lanes = 4 * windows_here
    here = lax.axis_index("tm").astype(jnp.int32)
    is_even = lax.axis_index("fiber") % 2 == 0

    pair_shape = jax.ShapeDtypeStruct((bins_here // 2, block, lanes), jnp.bfloat16)
    mine, other = pl.pallas_call(
        spectra_kernel,
        in_specs=[
            pl.BlockSpec(memory_space=pltpu.SMEM),
            pl.BlockSpec(memory_space=pltpu.HBM),
            pl.BlockSpec(memory_space=pltpu.HBM),
        ],
        out_specs=[pl.BlockSpec(memory_space=pltpu.VMEM)] * 2,
        out_shape=[pair_shape, pair_shape],
        scratch_shapes=[
            pltpu.VMEM((-(-block // LANES), windows_here * 2 * FREQS, LANES), jnp.float32),
            pltpu.VMEM((windows_here, block, length), jnp.bfloat16),
            pltpu.VMEM((2 * FREQS, length), jnp.bfloat16),
            pltpu.SemaphoreType.DMA((5,)),
        ],
        compiler_params=pltpu.CompilerParams(vmem_limit_bytes=60 << 20),
    )(
        jnp.stack([here, counts[0]]),
        samples,
        jnp.asarray(make_table(length, FREQS, FIRST_BIN)),
    )
    theirs = lax.ppermute(other, "tm", [(0, 1), (1, 0)])
    half = bins_here // 2
    quarter = half // 2
    half_shape = jax.ShapeDtypeStruct((half, block, lanes), jnp.bfloat16)
    own = pl.pallas_call(
        functools.partial(merge_kernel, total_windows=total_windows),
        in_specs=[pl.BlockSpec(memory_space=pltpu.VMEM)] * 2,
        out_specs=[pl.BlockSpec(memory_space=pltpu.VMEM)] * 2,
        out_shape=[half_shape] * 2,
        compiler_params=pltpu.CompilerParams(vmem_limit_bytes=32 << 20),
    )(mine, theirs)

    down = [(i, i - 2) for i in range(2, fiber_size)]
    down_odd = [(i, i - 2) for i in range(3, fiber_size, 2)]
    to_even = [(i, i - 1) for i in range(1, fiber_size, 2)]
    to_odd = [(i - 1, i) for i in range(1, fiber_size, 2)]

    def pick(for_even, for_odd):
        even_one, for_even, for_odd = lax.optimization_barrier((is_even, for_even, for_odd))
        return lax.optimization_barrier(jnp.where(even_one, for_even, for_odd))

    def send(payload, route):
        return lax.ppermute(payload, "fiber", route)

    def after(payload, *others):
        return lax.optimization_barrier((payload, *others))

    near_reach = 2 * block
    offsets = jnp.arange(1, near_reach + HOPS * LANES + 1, dtype=jnp.int32)
    mask = (offsets[None, :] <= reach_limit[:, None]).astype(jnp.bfloat16)
    masks = (mask[:, 2 * LANES : near_reach], mask[:, near_reach:])

    def near(outs, at, one, two):
        return band(
            at * half, half, 0, (own[at], 0), (one, two), masks[0], outs, bins_here, total_windows
        )

    def far(outs, at, first, bins, two, three):
        return band(
            at * half + first, bins, 1, (own[at], first), (two, three), masks[1], outs, bins_here,
            total_windows,
        )

    ahead_low = send(own[0], to_even)
    z_low = send(own[0], down)
    own_high, ahead_low, *masks = after(own[1], ahead_low, *masks)
    z_high = send(own_high, down)
    up_low = send(z_low, to_odd)
    ahead_high = send(own_high, to_even)
    up_high = send(z_high, to_odd)
    z_back, ahead_high = after(z_low, ahead_high)
    back_low = send(z_back, to_even)
    z_next = send(up_low, down_odd)
    outs = near(None, 0, ((ahead_low, 0), (up_low, 0)), ((z_low, 0), (z_low, 0)))
    up_high, *outs = after(up_high, *outs)
    last = [
        send(pick(ahead_high[at : at + quarter], up_high[at : at + quarter]), down)
        for at in (0, quarter)
    ]
    outs = near(outs, 1, ((ahead_high, 0), (up_high, 0)), ((z_high, 0), (z_high, 0)))
    outs = far(outs, 0, 0, half, ((z_low, 0), (z_low, 0)), ((back_low, 0), (z_next, 0)))
    for part, at in enumerate((0, quarter)):
        outs = far(
            outs, 1, at, quarter, ((z_high, at), (z_high, at)), ((last[part], 0), (last[part], 0))
        )
    return tuple(outs)


def solution(mesh):
    placed = (P("tm", ("grp", "fiber"), None), P(("grp", "fiber")), P(("grp", "fiber")))
    return jax.shard_map(
        body,
        mesh=mesh,
        in_specs=placed,
        out_specs=(P("tm", ("grp", "fiber"), None), P("tm", ("grp", "fiber"), None)),
        check_vma=False,
    )
```

```python
import functools
import math

import jax
import jax.numpy as jnp
import ml_dtypes
import numpy as np
from jax import lax
from jax.experimental import pallas as pl
from jax.experimental.pallas import tpu as pltpu
from jax.sharding import PartitionSpec as P

FREQS = 32
FIRST_BIN = 8
LANES = 128
HOPS = 3
ROWS = 64
AT_ONCE = 2
VMEM = 16 << 20


def make_table(length, bins, first_bin):
    steps_index = np.arange(length, dtype=np.int32)
    bin_index = np.arange(bins, dtype=np.int32) + first_bin
    products = bin_index[:, None] * steps_index[None, :] % length
    phases = (2.0 * math.pi * products / length).astype(np.float32)
    taper = 0.5 - 0.5 * np.cos((2.0 * math.pi * steps_index / length).astype(np.float32))
    taper = taper.astype(np.float32)
    cosines = taper[None, :] * np.cos(phases)
    sines = -taper[None, :] * np.sin(phases)
    return np.concatenate([cosines, sines], axis=0).astype(ml_dtypes.bfloat16)


def spectra_kernel(place_ref, samples_ref, table_ref, mine_ref, other_ref, raw_ref):
    windows, block, _ = samples_ref.shape
    pairs = mine_ref.shape[0]
    here = place_ref[0]
    tiles = raw_ref.shape[0]
    channel = lax.broadcasted_iota(jnp.int32, (1, block), 1)
    active = (channel < place_ref[1]).astype(jnp.float32)
    for w in range(windows):
        raw = lax.dot_general(
            table_ref[...], samples_ref[w], (((1,), (1,)), ((), ())),
            preferred_element_type=jnp.float32,
        )
        level = jnp.sum(raw * raw, axis=0, keepdims=True) * (1.0 / FREQS)
        white = raw * (lax.rsqrt(level + 1e-06) * active)
        for tile in range(tiles):
            start = tile * LANES
            width = min(LANES, block - start)
            raw_ref[tile, w * 2 * FREQS : (w + 1) * 2 * FREQS, :width] = white[:, start : start + width]
    for out_ref, first in ((mine_ref, here * 2 * pairs), (other_ref, (1 - here) * 2 * pairs)):
        for pair in range(pairs):
            for tile in range(tiles):
                start = tile * LANES
                width = min(LANES, block - start)
                rows = [
                    raw_ref[tile, pl.ds(first + 2 * pair + part, windows, stride=2 * FREQS), :]
                    for part in (0, FREQS, 1, FREQS + 1)
                ]
                turned = jnp.concatenate(rows, axis=0).T
                out_ref[pair, start : start + width, :] = turned[:width].astype(jnp.bfloat16)


def merge_kernel(mine_ref, theirs_ref, *out_refs, total_windows):
    block, lanes = mine_ref.shape[1:]
    half = lanes // 2
    lane = lax.broadcasted_iota(jnp.int32, (block, lanes), 1)
    per_chunk = out_refs[0].shape[0]
    for pair in range(mine_ref.shape[0]):
        mine = mine_ref[pair].astype(jnp.float32)
        theirs = theirs_ref[pair].astype(jnp.float32)
        both = (
            jnp.where(lane < half, mine, pltpu.roll(theirs, half, 1)),
            jnp.where(lane < half, pltpu.roll(mine, half, 1), theirs),
        )
        for step, values in enumerate(both):
            power = jnp.sum(values * values, axis=1, keepdims=True)
            root = lax.rsqrt(power * (1.0 / total_windows) + 1e-06)
            bin_at = 2 * pair + step
            out_refs[bin_at // per_chunk][bin_at % per_chunk] = (values * root).astype(jnp.bfloat16)


def band_kernel(*refs, own_first, places, hops, first_tile, total_windows):
    own_ref = refs[0]
    real_ref, _, right_ref, _ = refs[-4:]
    at_once, block, _ = real_ref.shape
    depth = right_ref.shape[2]
    start_bin = pl.program_id(0) * at_once
    origin = hops[0] * block
    filled = len(hops) * block
    parity = lax.rem(lax.axis_index("fiber"), 2)

    def gather(odd):
        for inner in range(at_once):
            for hop, place in zip([hop for hop in hops if hop], places):
                operand, first_bin = place[odd]
                start = hop * block - origin
                right_ref[inner, start : start + block] = refs[operand][
                    first_bin + start_bin + inner
                ]

    pl.when(parity == 0)(lambda: gather(0))
    pl.when(parity == 1)(lambda: gather(1))
    for inner in range(at_once):
        own = own_ref[own_first + start_bin + inner]
        if hops[0] == 0:
            right_ref[inner, :block] = own
        if right_ref.shape[1] > filled:
            padding = (right_ref.shape[1] - filled, depth)
            right_ref[inner, filled:] = jnp.zeros(padding, jnp.bfloat16)
        one_bin(refs, own, inner, hops, first_tile, total_windows)


def one_bin(refs, own, inner, hops, first_tile, total_windows):
    mask_ref = refs[1]
    real_ref, imag_ref, right_all, left_all = refs[-4:]
    right_ref, left_ref = right_all.at[inner], left_all.at[inner]
    block, depth = own.shape
    reach = min(HOPS * block - first_tile * LANES, real_ref.shape[2])
    origin = hops[0] * block
    wide = own.astype(jnp.float32) * (1.0 / math.sqrt(total_windows))
    part = depth // 4
    lane = lax.broadcasted_iota(jnp.int32, (block, depth), 1)
    turned = jnp.where(
        (lane // part) % 2 == 0, pltpu.roll(wide, depth - part, 1), -pltpu.roll(wide, part, 1)
    )
    for first in range(0, block, ROWS):
        count = min(ROWS, block - first)
        rows = slice(first, first + count)
        left_ref[2 * first : 2 * first + count] = wide[rows].astype(jnp.bfloat16)
        left_ref[2 * first + count : 2 * (first + count)] = turned[rows].astype(jnp.bfloat16)
    out_tiles = -(-reach // LANES)
    mask_from = 2 if first_tile == 0 else 0
    for first in range(0, block, ROWS):
        count = min(ROWS, block - first)
        lane_of = lax.broadcasted_iota(jnp.int32, (count, LANES), 1)
        row_of = lax.broadcasted_iota(jnp.int32, (count, LANES), 0)
        begin = first + 1 + first_tile * LANES - origin
        base = begin // LANES
        shift = begin - base * LANES + row_of
        tiles = (begin + count - 2 + reach) // LANES - base + 1
        products = lax.dot_general(
            left_ref[2 * first : 2 * (first + count)],
            right_ref[base * LANES : (base + tiles) * LANES],
            (((1,), (1,)), ((), ())),
            preferred_element_type=jnp.float32,
        )
        keep = lane_of >= shift
        source = (lane_of + shift) % LANES
        for out_at, out_ref in enumerate((real_ref, imag_ref)):
            rows = products[out_at * count : (out_at + 1) * count]
            for tile in range(out_tiles):
                start = tile * LANES
                width = min(LANES, reach - start)
                values = rows[:, start : start + LANES]
                if tile + 1 < tiles:
                    values = jnp.where(keep, values, rows[:, start + LANES : start + 2 * LANES])
                moved = jnp.take_along_axis(values, source, axis=1, mode="promise_in_bounds")
                moved = moved.astype(jnp.bfloat16)
                if tile >= mask_from:
                    column = (tile - mask_from) * LANES
                    moved = moved * mask_ref[first : first + count, column : column + LANES]
                out_ref[inner, first : first + count, start : start + width] = moved[:, :width]


def band(first_bin, bins, far, own, places, mask, so_far, bins_here, total_windows):
    _, block, depth = own[0].shape
    out = jax.ShapeDtypeStruct((bins_here, block, HOPS * block), jnp.bfloat16)
    near_width = 2 * block
    hops = (2, 3) if far else (0, 1, 2)
    out_spec = pl.BlockSpec(
        (AT_ONCE, block, near_width), lambda i: (first_bin // AT_ONCE + i, 0, 1 if far else 0)
    )
    operands = [own[0], mask]

    def index_of(array):
        for at, operand in enumerate(operands):
            if operand is array:
                return at
        operands.append(array)
        return len(operands) - 1

    places = [tuple((index_of(array), offset) for array, offset in place) for place in places]
    in_specs = [pl.BlockSpec(memory_space=pltpu.VMEM)] * len(operands)
    aliases = {}
    if so_far is not None:
        aliases = {len(operands): 0, len(operands) + 1: 1}
        operands += list(so_far)
        in_specs += [pl.BlockSpec(memory_space=pl.ANY)] * 2
    wide = block if far else near_width
    return pl.pallas_call(
        functools.partial(
            band_kernel,
            own_first=own[1],
            places=places,
            hops=hops,
            first_tile=near_width // LANES if far else 0,
            total_windows=total_windows,
        ),
        grid=(bins // AT_ONCE,),
        in_specs=in_specs,
        out_specs=[out_spec, out_spec],
        scratch_shapes=[
            pltpu.VMEM((AT_ONCE, -(-len(hops) * block // LANES) * LANES, depth), jnp.bfloat16),
            pltpu.VMEM((AT_ONCE, 2 * block, depth), jnp.bfloat16),
        ],
        out_shape=[out, out],
        input_output_aliases=aliases,
        cost_estimate=pl.CostEstimate(
            flops=bins * 4 * block * wide * depth,
            bytes_accessed=bins * 4 * block * wide,
            transcendentals=0,
        ),
        compiler_params=pltpu.CompilerParams(vmem_limit_bytes=VMEM),
    )(*operands)


def body(samples, counts, reach_limit):
    windows_here, block, length = samples.shape
    tm_size = lax.axis_size("tm")
    fiber_size = lax.axis_size("fiber")
    total_windows = windows_here * tm_size
    bins_here = FREQS // tm_size
    lanes = 4 * windows_here
    here = lax.axis_index("tm").astype(jnp.int32)
    is_even = lax.axis_index("fiber") % 2 == 0

    pair_shape = jax.ShapeDtypeStruct((bins_here // 2, block, lanes), jnp.bfloat16)
    mine, other = pl.pallas_call(
        spectra_kernel,
        in_specs=[
            pl.BlockSpec(memory_space=pltpu.SMEM),
            pl.BlockSpec(memory_space=pltpu.VMEM),
            pl.BlockSpec(memory_space=pltpu.VMEM),
        ],
        out_specs=[pl.BlockSpec(memory_space=pltpu.VMEM)] * 2,
        out_shape=[pair_shape, pair_shape],
        scratch_shapes=[
            pltpu.VMEM((-(-block // LANES), windows_here * 2 * FREQS, LANES), jnp.float32)
        ],
        compiler_params=pltpu.CompilerParams(vmem_limit_bytes=VMEM),
    )(
        jnp.stack([here, counts[0]]),
        samples,
        jnp.asarray(make_table(length, FREQS, FIRST_BIN)),
    )
    theirs = lax.ppermute(other, "tm", [(0, 1), (1, 0)])
    half = bins_here // 2
    quarter = half // 2
    half_shape = jax.ShapeDtypeStruct((half, block, lanes), jnp.bfloat16)
    own = pl.pallas_call(
        functools.partial(merge_kernel, total_windows=total_windows),
        in_specs=[pl.BlockSpec(memory_space=pltpu.VMEM)] * 2,
        out_specs=[pl.BlockSpec(memory_space=pltpu.VMEM)] * 2,
        out_shape=[half_shape] * 2,
        compiler_params=pltpu.CompilerParams(vmem_limit_bytes=32 << 20),
    )(mine, theirs)

    down = [(i, i - 2) for i in range(2, fiber_size)]
    down_odd = [(i, i - 2) for i in range(3, fiber_size, 2)]
    to_even = [(i, i - 1) for i in range(1, fiber_size, 2)]
    to_odd = [(i - 1, i) for i in range(1, fiber_size, 2)]

    def pick(for_even, for_odd):
        even_one, for_even, for_odd = lax.optimization_barrier((is_even, for_even, for_odd))
        return lax.optimization_barrier(jnp.where(even_one, for_even, for_odd))

    def send(payload, route):
        return lax.ppermute(payload, "fiber", route)

    def after(payload, *others):
        return lax.optimization_barrier((payload, *others))

    near_reach = 2 * block
    offsets = jnp.arange(1, near_reach + HOPS * LANES + 1, dtype=jnp.int32)
    mask = (offsets[None, :] <= reach_limit[:, None]).astype(jnp.bfloat16)
    masks = (mask[:, 2 * LANES : near_reach], mask[:, near_reach:])

    def near(outs, at, one, two):
        return band(
            at * half, half, 0, (own[at], 0), (one, two), masks[0], outs, bins_here, total_windows
        )

    def far(outs, at, first, bins, two, three):
        return band(
            at * half + first, bins, 1, (own[at], first), (two, three), masks[1], outs, bins_here,
            total_windows,
        )

    ahead_low = send(own[0], to_even)
    z_low = send(own[0], down)
    own_high, ahead_low, *masks = after(own[1], ahead_low, *masks)
    z_high = send(own_high, down)
    up_low = send(z_low, to_odd)
    ahead_high = send(own_high, to_even)
    up_high = send(z_high, to_odd)
    z_back, ahead_high = after(z_low, ahead_high)
    back_low = send(z_back, to_even)
    z_next = send(up_low, down_odd)
    outs = near(None, 0, ((ahead_low, 0), (up_low, 0)), ((z_low, 0), (z_low, 0)))
    up_high, *outs = after(up_high, *outs)
    last = [
        send(pick(ahead_high[at : at + quarter], up_high[at : at + quarter]), down)
        for at in (0, quarter)
    ]
    outs = near(outs, 1, ((ahead_high, 0), (up_high, 0)), ((z_high, 0), (z_high, 0)))
    outs = far(outs, 0, 0, half, ((z_low, 0), (z_low, 0)), ((back_low, 0), (z_next, 0)))
    for part, at in enumerate((0, quarter)):
        outs = far(
            outs, 1, at, quarter, ((z_high, at), (z_high, at)), ((last[part], 0), (last[part], 0))
        )
    return tuple(outs)


def solution(mesh):
    placed = (P("tm", ("grp", "fiber"), None), P(("grp", "fiber")), P(("grp", "fiber")))
    return jax.shard_map(
        body,
        mesh=mesh,
        in_specs=placed,
        out_specs=(P("tm", ("grp", "fiber"), None), P("tm", ("grp", "fiber"), None)),
        check_vma=False,
    )
```
